32 devices in a mesh: member: 8 (over z, y), dp: 4 (over x, core).
Axes of the slice: x: 2, y: 2, z: 4, core: 2. Of those that a mesh axis runs over, the one named last changes fastest.
Arguments:
- tokens: bfloat16 [8, 16, 196, 768], P('member', 'dp'), may hold values from -6 to 6
- labels: int32 [8, 16], P('member', 'dp'), may hold values from 0 to 499
- source: int32 [8], replicated, may hold values from 0 to 7, as said below
- learn_rate: float32 [8], P('member'), may hold values from 0.02 to 0.2
- weight_decay: float32 [8], P('member'), may hold values from 0.1 to 1
- classifier: bfloat16 [768, 500], replicated, may hold values from -8 to 8
- up_param: float32 [8, 768, 1536], P('member', 'dp'), may hold values from -6 to 6
- up_first: bfloat16 [8, 768, 1536], P('member', 'dp'), may hold values from -0.005859375 to 0.005859375
- up_second: float32 [8, 768, 1536], P('member', 'dp'), may hold values from 1e-07 to 1e-05
- down_param: float32 [8, 1536, 768], P('member', 'dp'), may hold values from -6 to 6
- down_first: bfloat16 [8, 1536, 768], P('member', 'dp'), may hold values from -0.005859375 to 0.005859375
- down_second: float32 [8, 1536, 768], P('member', 'dp'), may hold values from 1e-07 to 1e-05
Outputs:
- up_weight: float32 [8, 768, 1536], P('member', 'dp')
- up_moment: bfloat16 [8, 768, 1536], P('member', 'dp')
- up_variance: float32 [8, 768, 1536], P('member', 'dp')
- down_weight: float32 [8, 1536, 768], P('member', 'dp')
- down_moment: bfloat16 [8, 1536, 768], P('member', 'dp')
- down_variance: float32 [8, 1536, 768], P('member', 'dp')
The draws below stay inside these ranges and needn't reach their ends.
Inputs may be any that keep to these rules, and one draw needn't show every extreme that they name: source[i] = i except for the 2 members of the lowest quartile of a ranking; each of those names a member of the highest quartile, which keeps its own index; a winner may be named by several losers.
All inputs are finite; a program needn't handle non-finite values.
Results may differ from the reference program's by a relative error of at most 0.009.
Values may be sent and summed in bfloat16 or wider, within the bound.
No kernel may reach another device: no remote copies, remote signals or barrier semaphores. Data moves between devices by JAX's collectives and lax.ppermute only.
A program may use at most 128 MiB of HBM per device.

```python
import math
import jax
import jax.numpy as jnp
from jax import lax

D = 768
FF = 1536
CLASSES = 500
PATCHES = 196
IMG_DEV = 4
STEP = 1000
MEMBERS = 8
BATCH = 16
N_DP = 4


def draw_source(key, part):
    ranking = jax.random.permutation(jax.random.fold_in(key, 11), MEMBERS).astype(jnp.int32)
    quarter = MEMBERS // 4
    winners = ranking[:quarter]
    losers = ranking[MEMBERS - quarter:]
    picks = jax.random.randint(jax.random.fold_in(key, 12), (quarter,), 0, quarter)
    mapping = jnp.arange(MEMBERS, dtype=jnp.int32)
    return mapping.at[losers].set(winners[picks]).astype(jnp.int32)


def set_ends(result, rng, smallest, top_value):
    longest = result.shape.index(max(result.shape))
    spots = []
    for shift in (0, 1):
        where = [jax.random.randint(jax.random.fold_in(rng, axis), (), 0, length) for axis, length in enumerate(result.shape)]
        where[longest] = (where[longest] + shift) % result.shape[longest]
        spots.append(tuple(where))
    return result.at[spots[0]].set(smallest).at[spots[1]].set(top_value)


def block_levels(stream_key, dims, shards, least, high):
    loudness, own = 1.0, jax.random.fold_in(stream_key, 6)
    for position, parts in shards:
        heights = jnp.exp(jax.random.uniform(jax.random.fold_in(own, position), (parts,), jnp.float32, least / len(shards), high / len(shards)))
        loudness = loudness * jnp.repeat(heights, dims[position] // parts).reshape([-1 if axis == position else 1 for axis in range(len(dims))])
    return loudness


def noise(rng, shape, deviation, bound, pieces=(), held_as=jnp.bfloat16):
    result = deviation * jax.random.normal(rng, shape, jnp.float32)
    if pieces:
        result = result * block_levels(rng, shape, pieces, -0.22, 0.18)
    return jnp.clip(result, -bound, bound).astype(held_as)


def setup_inputs(seed: int = 0) -> dict:
    arg_keys = jax.random.split(jax.random.key(seed), 13)
    tokens = noise(arg_keys[0], (MEMBERS, BATCH, PATCHES, D), 1.0, 6.0, ((0, 8), (1, 4)))
    labels = set_ends(jax.random.randint(arg_keys[1], (MEMBERS, BATCH), 0, CLASSES), jax.random.fold_in(arg_keys[1], 1), 0, CLASSES - 1).astype(jnp.int32)
    source = draw_source(jax.random.fold_in(arg_keys[12], 71), 0)
    learn_rate = jnp.clip(jnp.exp(math.log(0.2) - 2.3025851 * jax.random.uniform(arg_keys[3], (MEMBERS,), jnp.float32) ** block_levels(arg_keys[3], (MEMBERS,), ((0, 8),), -0.2, 0.2)), 0.02, 0.2)
    weight_decay = jnp.clip(jnp.exp(math.log(1.0) - 2.3025851 * jax.random.uniform(arg_keys[4], (MEMBERS,), jnp.float32) ** block_levels(arg_keys[4], (MEMBERS,), ((0, 8),), -0.2, 0.2)), 0.1, 1.0)
    classifier = noise(arg_keys[5], (D, CLASSES), 1.5, 8.0)
    up_param = noise(arg_keys[6], (MEMBERS, D, FF), 1.0, 6.0, ((0, 8), (1, 4)), jnp.float32)
    up_first = noise(arg_keys[7], (MEMBERS, D, FF), 0.001, 0.005859375, ((0, 8), (1, 4)))
    up_second = jnp.clip(jnp.exp(math.log(9.999999747378752e-06) - 4.6051701 * jax.random.uniform(arg_keys[8], (MEMBERS, D, FF), jnp.float32) ** block_levels(arg_keys[8], (MEMBERS, D, FF), ((0, 8), (1, 4)), -0.2, 0.2)), 1.0000000116860974e-07, 9.999999747378752e-06)
    down_param = noise(arg_keys[9], (MEMBERS, FF, D), 1.0, 6.0, ((0, 8), (1, 4)), jnp.float32)
    down_first = noise(arg_keys[10], (MEMBERS, FF, D), 0.001, 0.005859375, ((0, 8), (1, 4)))
    down_second = jnp.clip(jnp.exp(math.log(9.999999747378752e-06) - 4.6051701 * jax.random.uniform(arg_keys[11], (MEMBERS, FF, D), jnp.float32) ** block_levels(arg_keys[11], (MEMBERS, FF, D), ((0, 8), (1, 4)), -0.2, 0.2)), 1.0000000116860974e-07, 9.999999747378752e-06)
    return dict(tokens=tokens, labels=labels, source=source, learn_rate=learn_rate, weight_decay=weight_decay, classifier=classifier, up_param=up_param, up_first=up_first, up_second=up_second, down_param=down_param, down_first=down_first, down_second=down_second)


def local_gradients(tokens, labels, up_weight, down_weight, classifier, batch_total):
    images, patches, features = tokens.shape
    hidden_units = up_weight.shape[1]
    token_rows = tokens.reshape(images * patches, features).astype(jnp.float32)
    center = token_rows - lax.optimization_barrier(jnp.mean(token_rows, axis=1, keepdims=True))
    normed = (center * lax.rsqrt(lax.optimization_barrier(jnp.mean(center * center, axis=1, keepdims=True)) + 1e-06)).astype(jnp.bfloat16)
    preact = jnp.dot(normed, up_weight, preferred_element_type=jnp.float32) * features ** (-0.5)
    activated = (0.5 * preact * (1.0 + lax.erf(preact * 0.7071067811865476))).astype(jnp.bfloat16)
    residual = token_rows + jnp.dot(activated, down_weight, preferred_element_type=jnp.float32) * hidden_units ** (-0.5)
    out_center = residual - lax.optimization_barrier(jnp.mean(residual, axis=1, keepdims=True))
    inverse = lax.rsqrt(lax.optimization_barrier(jnp.mean(out_center * out_center, axis=1, keepdims=True)) + 1e-06)
    out_normed = out_center * inverse
    pooled = lax.optimization_barrier(jnp.mean(out_normed.reshape(images, patches, features), axis=1)).astype(jnp.bfloat16)
    logits = jnp.dot(pooled, classifier, preferred_element_type=jnp.float32)
    powered = jnp.exp(logits)
    softmax_out = powered / lax.optimization_barrier(jnp.sum(powered, axis=1, keepdims=True))
    onehot = (labels[:, None] == jnp.arange(classifier.shape[1], dtype=jnp.int32)[None, :]).astype(jnp.float32)
    logit_delta = ((softmax_out - onehot) / batch_total).astype(jnp.bfloat16)
    pool_delta = lax.dot_general(logit_delta, classifier, (((1,), (1,)), ((), ())), preferred_element_type=jnp.float32) / patches
    token_delta = jnp.broadcast_to(pool_delta[:, None, :], (images, patches, features)).reshape(images * patches, features)
    residual_delta = inverse * (token_delta - lax.optimization_barrier(jnp.mean(token_delta, axis=1, keepdims=True)) - out_normed * lax.optimization_barrier(jnp.mean(token_delta * out_normed, axis=1, keepdims=True)))
    residual_delta = residual_delta.astype(jnp.bfloat16)
    down_scale = hidden_units ** (-0.5)
    down_gradient = lax.dot_general(activated, residual_delta, (((0,), (0,)), ((), ())), preferred_element_type=jnp.float32) * down_scale
    hidden_delta = lax.dot_general(residual_delta, down_weight, (((1,), (1,)), ((), ())), preferred_element_type=jnp.float32) * down_scale
    derivative = 0.5 * (1.0 + lax.erf(preact * 0.7071067811865476)) + preact * jnp.exp(-0.5 * preact * preact) * 0.3989422804014327
    preact_delta = (hidden_delta * derivative).astype(jnp.bfloat16)
    up_gradient = lax.dot_general(normed, preact_delta, (((0,), (0,)), ((), ())), preferred_element_type=jnp.float32) * features ** (-0.5)
    return (up_gradient, down_gradient)

def adamw_step(param, first, second, gradient, rate_value, decay_value):
    moment = 0.9 * first.astype(jnp.float32) + 0.1 * gradient
    variance = 0.999 * second + 0.001 * gradient * gradient
    update = moment / (1.0 - 0.9 ** STEP) / (jnp.sqrt(variance / (1.0 - 0.999 ** STEP)) + 1e-08) + decay_value * param
    return (param - rate_value * update, moment.astype(jnp.bfloat16), variance)

def reference(tokens, labels, source, learn_rate, weight_decay, classifier, up_param, up_first, up_second, down_param, down_first, down_second):

    def member_update(index):
        winner = source[index]

        def chosen(array):
            return lax.dynamic_index_in_dim(array, winner, 0, keepdims=False)
        up_now, up_mom, up_var = (chosen(up_param), chosen(up_first), chosen(up_second))
        down_now, down_mom, down_var = (chosen(down_param), chosen(down_first), chosen(down_second))
        up_bf = up_now.astype(jnp.bfloat16)
        down_bf = down_now.astype(jnp.bfloat16)
        member_tokens = lax.dynamic_index_in_dim(tokens, index, 0, keepdims=False)
        member_labels = lax.dynamic_index_in_dim(labels, index, 0, keepdims=False)
        up_total = jnp.zeros((D, FF), jnp.float32)
        down_total = jnp.zeros((FF, D), jnp.float32)
        for group in range(N_DP):
            first_grad, second_grad = local_gradients(member_tokens[group * IMG_DEV:(group + 1) * IMG_DEV], member_labels[group * IMG_DEV:(group + 1) * IMG_DEV], up_bf, down_bf, classifier, BATCH)
            up_total = up_total + lax.optimization_barrier(first_grad.astype(jnp.bfloat16)).astype(jnp.float32)
            down_total = down_total + lax.optimization_barrier(second_grad.astype(jnp.bfloat16)).astype(jnp.float32)
        rate_value = learn_rate[index]
        decay_value = weight_decay[index]
        up_new = adamw_step(up_now, up_mom, up_var, up_total, rate_value, decay_value)
        down_new = adamw_step(down_now, down_mom, down_var, down_total, rate_value, decay_value)
        return up_new + down_new
    results = lax.map(member_update, jnp.arange(MEMBERS, dtype=jnp.int32))
    return (results[0], results[1], results[2], results[3], results[4], results[5])
```

```python
import jax
import jax.numpy as jnp
from jax import lax
from jax.sharding import PartitionSpec as P

STEP = 1000
DIRECT_MEMBERS = 8
F32 = jnp.float32
BF16 = jnp.bfloat16


def after(value, token):
    return lax.optimization_barrier((value, token))[0]


def pairs_of(members):
    return [(winner, loser) for loser in range(members) for winner in range(members) if winner != loser]


def find_slots(source):
    members = source.shape[0]
    index = jnp.arange(members, dtype=jnp.int32)
    loses = source != index
    place = index * (members - 1) + jnp.where(source < index, source, source - 1)
    top = members * members
    first = jnp.min(jnp.where(loses, place, top))
    last = jnp.max(jnp.where(loses, place, -1))
    return first, last


def take_direct(arrays, slots, me, members):
    def branch(pair):
        return lambda parts: tuple(lax.ppermute(part, "member", [pair]) for part in parts)

    branches = [branch(pair) for pair in pairs_of(members)]
    first, last = slots
    got_first = lax.switch(first, branches, arrays)
    got_last = lax.switch(last, branches, after(arrays, got_first))
    is_first = me == first // (members - 1)
    is_last = me == last // (members - 1)
    return tuple(
        jnp.where(is_first, one, jnp.where(is_last, two, own))
        for own, one, two in zip(arrays, got_first, got_last)
    )


def take_through_all(arrays, source, members):
    def move(array):
        flat = array.reshape(members, -1)
        parts = lax.all_to_all(flat, "member", split_axis=0, concat_axis=0, tiled=True)
        picked = jnp.take(parts, source, axis=0)
        return lax.all_to_all(picked, "member", split_axis=0, concat_axis=0, tiled=True).reshape(array.shape)

    return tuple(move(array) for array in arrays)


def swap_core(value):
    return lax.ppermute(value, "dp", [(0, 1), (1, 0), (2, 3), (3, 2)])


def swap_chip(value):
    return lax.ppermute(value, "dp", [(0, 2), (2, 0), (1, 3), (3, 1)])


def gather_rows(own, chip, core):
    far = swap_chip(own)
    near = swap_core(own)
    diagonal = swap_core(far)
    on_zero = jnp.where(core == 0, jnp.stack([own, near]), jnp.stack([near, own]))
    on_one = jnp.where(core == 0, jnp.stack([far, diagonal]), jnp.stack([diagonal, far]))
    both = jnp.where(chip == 0, jnp.stack([on_zero, on_one]), jnp.stack([on_one, on_zero]))
    return both.reshape(4 * own.shape[0], own.shape[1])


def sum_rows(terms, chip, core):
    rows = terms.shape[0] // 4
    split = terms.reshape(2, 2, rows, terms.shape[1])
    mine = lax.dynamic_index_in_dim(split, core, 1, False)
    theirs = lax.dynamic_index_in_dim(split, 1 - core, 1, False)
    chip_sum = mine.astype(F32) + swap_core(theirs).astype(F32)
    away = lax.dynamic_index_in_dim(chip_sum, 1 - chip, 0, False).astype(BF16)
    home = lax.dynamic_index_in_dim(chip_sum, chip, 0, False)
    return home + swap_chip(away).astype(F32)


def adamw_step(param, first, second, gradient, rate_value, decay_value):
    moment = 0.9 * first.astype(F32) + 0.1 * gradient
    variance = 0.999 * second + 0.001 * gradient * gradient
    update = (
        moment / (1.0 - 0.9**STEP) / (jnp.sqrt(variance / (1.0 - 0.999**STEP)) + 1e-08)
        + decay_value * param
    )
    return (param - rate_value * update, moment.astype(BF16), variance)


def per_device(
    tokens,
    labels,
    source,
    learn_rate,
    weight_decay,
    classifier,
    up_param,
    up_first,
    up_second,
    down_param,
    down_first,
    down_second,
):
    members = lax.axis_size("member")
    shards = lax.axis_size("dp")
    me = lax.axis_index("member")
    place = lax.axis_index("dp")
    chip, core = place // 2, place % 2
    tokens, labels = tokens[0], labels[0]
    up_param, up_first, up_second = up_param[0], up_first[0], up_second[0]
    down_param, down_first, down_second = down_param[0], down_first[0], down_second[0]
    loses = source[me] != me

    if members == DIRECT_MEMBERS:
        slots = find_slots(source)

        def take(arrays, token):
            return take_direct(after(arrays, token), slots, me, members)
    else:

        def take(arrays, token):
            return take_through_all(after(arrays, token), source, members)

    (up_short,) = take((up_param.astype(BF16),), ())
    (down_short,) = take((down_param.astype(BF16),), up_short)
    up_full = gather_rows(up_short, chip, core)
    down_full = gather_rows(down_short, chip, core)
    moments = take((up_first, down_first), down_short)

    images, patches, features = tokens.shape
    hidden_units = up_full.shape[1]
    batch_total = images * shards
    token_rows = tokens.reshape(images * patches, features).astype(F32)
    center = token_rows - jnp.mean(token_rows, axis=1, keepdims=True)
    normed = (center * lax.rsqrt(jnp.mean(center * center, axis=1, keepdims=True) + 1e-06)).astype(BF16)
    preact = jnp.dot(normed, up_full, preferred_element_type=F32) * features ** (-0.5)
    activated = (0.5 * preact * (1.0 + lax.erf(preact * 0.7071067811865476))).astype(BF16)
    down_scale = hidden_units ** (-0.5)
    residual = token_rows + jnp.dot(activated, down_full, preferred_element_type=F32) * down_scale
    out_center = residual - jnp.mean(residual, axis=1, keepdims=True)
    inverse = lax.rsqrt(jnp.mean(out_center * out_center, axis=1, keepdims=True) + 1e-06)
    out_normed = out_center * inverse
    pooled = jnp.mean(out_normed.reshape(images, patches, features), axis=1).astype(BF16)
    logits = jnp.dot(pooled, classifier, preferred_element_type=F32)
    powered = jnp.exp(logits)
    softmax_out = powered / jnp.sum(powered, axis=1, keepdims=True)
    onehot = (labels[:, None] == jnp.arange(classifier.shape[1], dtype=jnp.int32)[None, :]).astype(F32)
    logit_delta = ((softmax_out - onehot) / batch_total).astype(BF16)
    pool_delta = (
        lax.dot_general(logit_delta, classifier, (((1,), (1,)), ((), ())), preferred_element_type=F32)
        / patches
    )
    token_delta = jnp.broadcast_to(pool_delta[:, None, :], (images, patches, features)).reshape(
        images * patches, features
    )
    residual_delta = inverse * (
        token_delta
        - jnp.mean(token_delta, axis=1, keepdims=True)
        - out_normed * jnp.mean(token_delta * out_normed, axis=1, keepdims=True)
    )
    residual_delta = residual_delta.astype(BF16)
    down_gradient = (
        lax.dot_general(activated, residual_delta, (((0,), (0,)), ((), ())), preferred_element_type=F32)
        * down_scale
    ).astype(BF16)
    down_share = sum_rows(down_gradient, chip, core)
    hidden_delta = (
        lax.dot_general(residual_delta, down_full, (((1,), (1,)), ((), ())), preferred_element_type=F32)
        * down_scale
    )
    derivative = (
        0.5 * (1.0 + lax.erf(preact * 0.7071067811865476))
        + preact * jnp.exp(-0.5 * preact * preact) * 0.3989422804014327
    )
    preact_delta = (hidden_delta * derivative).astype(BF16)
    up_gradient = (
        lax.dot_general(normed, preact_delta, (((0,), (0,)), ((), ())), preferred_element_type=F32)
        * features ** (-0.5)
    ).astype(BF16)
    up_share = sum_rows(up_gradient, chip, core)
    variances = take((up_second.astype(BF16), down_second.astype(BF16)), (moments, up_gradient))

    def kept(own, short):
        return jnp.where(loses, short.astype(F32), own)

    rate_value = learn_rate[0]
    decay_value = weight_decay[0]
    up_new = adamw_step(
        kept(up_param, up_short), moments[0], kept(up_second, variances[0]), up_share, rate_value, decay_value
    )
    down_new = adamw_step(
        kept(down_param, down_short), moments[1], kept(down_second, variances[1]), down_share, rate_value, decay_value
    )
    return tuple(part[None] for part in up_new + down_new)


def solution(mesh):
    rows = P("member", "dp", None)
    placed = (
        P("member", "dp", None, None),
        P("member", "dp"),
        P(),
        P("member"),
        P("member"),
        P(),
        rows,
        rows,
        rows,
        rows,
        rows,
        rows,
    )
    return jax.shard_map(per_device, mesh=mesh, in_specs=placed, out_specs=(rows,) * 6, check_vma=False)
```

```python
import jax
import jax.numpy as jnp
from jax import lax
from jax.sharding import PartitionSpec as P

STEP = 1000
DIRECT_MEMBERS = 8
F32 = jnp.float32
BF16 = jnp.bfloat16


def after(value, token):
    return lax.optimization_barrier((value, token))[0]


def pairs_of(members):
    return [(one, two) for one in range(members) for two in range(one + 1, members)]


def find_slots(source):
    members = source.shape[0]
    index = jnp.arange(members, dtype=jnp.int32)
    low, high = jnp.minimum(source, index), jnp.maximum(source, index)
    pair = low * (2 * members - 1 - low) // 2 + high - low - 1
    place = jnp.where(source != index, index * members * members + pair, -1)
    last = jnp.max(place)
    first = jnp.max(jnp.where(place == last, -1, place))
    return first, last


def take_direct(value, slots, me, members):
    def branch(one, two):
        return lambda part: lax.ppermute(part, "member", [(one, two), (two, one)])

    branches = [branch(one, two) for one, two in pairs_of(members)]
    square = members * members
    first, last = slots
    got_first = lax.switch(first % square, branches, value)
    got_last = lax.switch(last % square, branches, after(value, got_first))
    return jnp.where(
        me == first // square, got_first, jnp.where(me == last // square, got_last, value)
    )


def take_through_all(value, source, members):
    flat = value.reshape(members, -1)
    parts = lax.all_to_all(flat, "member", split_axis=0, concat_axis=0, tiled=True)
    picked = jnp.take(parts, source, axis=0)
    return lax.all_to_all(picked, "member", split_axis=0, concat_axis=0, tiled=True).reshape(value.shape)


def swap_core(value):
    return lax.ppermute(value, "dp", [(0, 1), (1, 0), (2, 3), (3, 2)])


def swap_chip(value):
    return lax.ppermute(value, "dp", [(0, 2), (2, 0), (1, 3), (3, 1)])


def gather_rows(own, chip, core):
    far = swap_chip(own)
    near = swap_core(own)
    diagonal = swap_core(far)
    on_zero = jnp.where(core == 0, jnp.stack([own, near]), jnp.stack([near, own]))
    on_one = jnp.where(core == 0, jnp.stack([far, diagonal]), jnp.stack([diagonal, far]))
    both = jnp.where(chip == 0, jnp.stack([on_zero, on_one]), jnp.stack([on_one, on_zero]))
    return both.reshape(4 * own.shape[0], own.shape[1])


def sum_rows(terms, chip, core):
    rows = terms.shape[0] // 4
    split = terms.reshape(2, 2, rows, terms.shape[1])
    mine = lax.dynamic_index_in_dim(split, core, 1, False)
    theirs = lax.dynamic_index_in_dim(split, 1 - core, 1, False)
    chip_sum = mine.astype(F32) + swap_core(theirs).astype(F32)
    away = lax.dynamic_index_in_dim(chip_sum, 1 - chip, 0, False).astype(BF16)
    home = lax.dynamic_index_in_dim(chip_sum, chip, 0, False)
    return home + swap_chip(away).astype(F32)


def adamw_step(param, first, second, gradient, rate_value, decay_value):
    moment = 0.9 * first.astype(F32) + 0.1 * gradient
    variance = 0.999 * second + 0.001 * gradient * gradient
    update = (
        moment / (1.0 - 0.9**STEP) / (jnp.sqrt(variance / (1.0 - 0.999**STEP)) + 1e-08)
        + decay_value * param
    )
    return (param - rate_value * update, moment.astype(BF16), variance)


def per_device(
    tokens,
    labels,
    source,
    learn_rate,
    weight_decay,
    classifier,
    up_param,
    up_first,
    up_second,
    down_param,
    down_first,
    down_second,
):
    members = lax.axis_size("member")
    shards = lax.axis_size("dp")
    me = lax.axis_index("member")
    place = lax.axis_index("dp")
    chip, core = place // 2, place % 2
    tokens, labels = tokens[0], labels[0]
    up_param, up_first, up_second = up_param[0], up_first[0], up_second[0]
    down_param, down_first, down_second = down_param[0], down_first[0], down_second[0]
    loses = source[me] != me

    if members == DIRECT_MEMBERS:
        slots = find_slots(source)

        def take(value, token):
            return take_direct(after(value, token), slots, me, members)
    else:

        def take(value, token):
            return take_through_all(after(value, token), source, members)

    up_short = take(up_param.astype(BF16), ())
    down_short = take(down_param.astype(BF16), up_short)
    up_full = gather_rows(up_short, chip, core)
    down_full = gather_rows(down_short, chip, core)
    up_state = take(jnp.stack([up_first, up_second.astype(BF16)]), down_short)

    images, patches, features = tokens.shape
    hidden_units = up_full.shape[1]
    batch_total = images * shards
    token_rows = tokens.reshape(images * patches, features).astype(F32)
    center = token_rows - jnp.mean(token_rows, axis=1, keepdims=True)
    normed = (center * lax.rsqrt(jnp.mean(center * center, axis=1, keepdims=True) + 1e-06)).astype(BF16)
    preact = jnp.dot(normed, up_full, preferred_element_type=F32) * features ** (-0.5)
    activated = (0.5 * preact * (1.0 + lax.erf(preact * 0.7071067811865476))).astype(BF16)
    down_scale = hidden_units ** (-0.5)
    residual = token_rows + jnp.dot(activated, down_full, preferred_element_type=F32) * down_scale
    out_center = residual - jnp.mean(residual, axis=1, keepdims=True)
    inverse = lax.rsqrt(jnp.mean(out_center * out_center, axis=1, keepdims=True) + 1e-06)
    out_normed = out_center * inverse
    pooled = jnp.mean(out_normed.reshape(images, patches, features), axis=1).astype(BF16)
    logits = jnp.dot(pooled, classifier, preferred_element_type=F32)
    powered = jnp.exp(logits)
    softmax_out = powered / jnp.sum(powered, axis=1, keepdims=True)
    onehot = (labels[:, None] == jnp.arange(classifier.shape[1], dtype=jnp.int32)[None, :]).astype(F32)
    logit_delta = ((softmax_out - onehot) / batch_total).astype(BF16)
    pool_delta = (
        lax.dot_general(logit_delta, classifier, (((1,), (1,)), ((), ())), preferred_element_type=F32)
        / patches
    )
    token_delta = jnp.broadcast_to(pool_delta[:, None, :], (images, patches, features)).reshape(
        images * patches, features
    )
    residual_delta = inverse * (
        token_delta
        - jnp.mean(token_delta, axis=1, keepdims=True)
        - out_normed * jnp.mean(token_delta * out_normed, axis=1, keepdims=True)
    )
    residual_delta = residual_delta.astype(BF16)
    down_gradient = (
        lax.dot_general(activated, residual_delta, (((0,), (0,)), ((), ())), preferred_element_type=F32)
        * down_scale
    ).astype(BF16)
    down_share = sum_rows(down_gradient, chip, core)
    hidden_delta = (
        lax.dot_general(residual_delta, down_full, (((1,), (1,)), ((), ())), preferred_element_type=F32)
        * down_scale
    )
    derivative = (
        0.5 * (1.0 + lax.erf(preact * 0.7071067811865476))
        + preact * jnp.exp(-0.5 * preact * preact) * 0.3989422804014327
    )
    preact_delta = (hidden_delta * derivative).astype(BF16)
    up_gradient = (
        lax.dot_general(normed, preact_delta, (((0,), (0,)), ((), ())), preferred_element_type=F32)
        * features ** (-0.5)
    ).astype(BF16)
    up_share = sum_rows(up_gradient, chip, core)
    down_state = take(jnp.stack([down_first, down_second.astype(BF16)]), (up_state, up_gradient))

    def kept(own, short):
        return jnp.where(loses, short.astype(F32), own)

    rate_value = learn_rate[0]
    decay_value = weight_decay[0]
    up_new = adamw_step(
        kept(up_param, up_short), up_state[0], kept(up_second, up_state[1]), up_share, rate_value, decay_value
    )
    down_new = adamw_step(
        kept(down_param, down_short), down_state[0], kept(down_second, down_state[1]), down_share, rate_value, decay_value
    )
    return tuple(part[None] for part in up_new + down_new)


def solution(mesh):
    rows = P("member", "dp", None)
    placed = (
        P("member", "dp", None, None),
        P("member", "dp"),
        P(),
        P("member"),
        P("member"),
        P(),
        rows,
        rows,
        rows,
        rows,
        rows,
        rows,
    )
    return jax.shard_map(per_device, mesh=mesh, in_specs=placed, out_specs=(rows,) * 6, check_vma=False)
```

```python
import jax
import jax.numpy as jnp
from jax import lax
from jax.experimental import pallas as pl
from jax.experimental.pallas import tpu as pltpu
from jax.sharding import PartitionSpec as P

STEP = 1000
DIRECT_MEMBERS = 8
F32 = jnp.float32
BF16 = jnp.bfloat16


def after(value, token):
    return lax.optimization_barrier((value, token))[0]


def pairs_of(members):
    return [(one, two) for one in range(members) for two in range(one + 1, members)]


def plan_kernel(members, source_ref, me_ref, first, second, third, fourth, shared, is_one, loses):
    none = members * (members - 1) // 2

    def place_of(one, two):
        low, high = jnp.minimum(one, two), jnp.maximum(one, two)
        return jnp.right_shift(low * (2 * members - 1 - low), 1) + high - low - 1

    zero = jnp.int32(0)
    taker_one = taker_two = source_one = source_two = zero
    for index in range(members):
        own = source_ref[index]
        takes = own != index
        taker_two = jnp.where(takes, index, taker_two)
        source_two = jnp.where(takes, own, source_two)
        back = members - 1 - index
        own = source_ref[back]
        takes = own != back
        taker_one = jnp.where(takes, back, taker_one)
        source_one = jnp.where(takes, own, source_one)
    same = source_one == source_two
    first[0] = place_of(source_one, taker_one)
    second[0] = place_of(source_two, taker_two)
    third[0] = jnp.where(same, place_of(taker_one, taker_two), place_of(source_one, taker_one))
    fourth[0] = jnp.where(same, none, place_of(source_two, taker_two))
    shared[0] = jnp.where(same, 1, 0)
    me = me_ref[0]
    is_one[0] = jnp.where(me == taker_one, 1, 0)
    loses[0] = jnp.where((me == taker_one) | (me == taker_two), 1, 0)


def find_plan(source, me):
    members = source.shape[0]
    scalars = pl.pallas_call(
        lambda *refs: plan_kernel(members, *refs),
        out_shape=[jax.ShapeDtypeStruct((1,), jnp.int32)] * 7,
        in_specs=[pl.BlockSpec(memory_space=pltpu.SMEM)] * 2,
        out_specs=[pl.BlockSpec(memory_space=pltpu.SMEM)] * 7,
    )(source, me.reshape(1))
    first, second, third, fourth, shared, is_one, loses = (scalar.reshape(()) for scalar in scalars)
    return first, second, third, fourth, shared == 1, is_one == 1, loses == 1


def swap_pair(value, place, members):
    def branch(one, two):
        return lambda part: lax.ppermute(part, "member", [(one, two), (two, one)])

    return lax.switch(place, [branch(one, two) for one, two in pairs_of(members)] + [lambda part: part], value)


def exchange_start(upper, lower, plan, members):
    first, second, _, _, shared = plan[:5]
    to_one = swap_pair(upper, first, members)
    to_two = swap_pair(after(jnp.where(shared, lower, upper), to_one), second, members)
    return to_one, to_two


def exchange_finish(upper, lower, halves, plan, members):
    to_one, to_two = halves
    _, _, third, fourth, shared, is_one, _ = plan
    to_third = swap_pair(jnp.where(shared, jnp.where(is_one, to_one, to_two), lower), third, members)
    to_fourth = swap_pair(after(lower, to_third), fourth, members)
    return (
        jnp.where(is_one, to_one, jnp.where(shared, to_third, to_two)),
        jnp.where(is_one, to_third, jnp.where(shared, to_two, to_fourth)),
    )


def wide(value):
    half = value.shape[0] // 2
    return jnp.concatenate([value[:half], value[half:]], axis=1)


def narrow(value):
    half = value.shape[1] // 2
    return jnp.concatenate([value[:, :half], value[:, half:]], axis=0)


def take_through_all(value, source, members):
    flat = value.reshape(members, -1)
    parts = lax.all_to_all(flat, "member", split_axis=0, concat_axis=0, tiled=True)
    picked = jnp.take(parts, source, axis=0)
    return lax.all_to_all(picked, "member", split_axis=0, concat_axis=0, tiled=True).reshape(value.shape)


def swap_core(value):
    return lax.ppermute(value, "dp", [(0, 1), (1, 0), (2, 3), (3, 2)])


def swap_chip(value):
    return lax.ppermute(value, "dp", [(0, 2), (2, 0), (1, 3), (3, 1)])


def place_rows(own, near, far, diagonal, place):
    full = jnp.zeros((4,) + own.shape, own.dtype)
    for step, block in enumerate((own, near, far, diagonal)):
        full = lax.dynamic_update_index_in_dim(full, block, place ^ step, 0)
    return full.reshape(4 * own.shape[0], own.shape[1])


def sum_in_chip(terms, chip, core):
    rows = terms.shape[0] // 4
    split = terms.reshape(2, 2, rows, terms.shape[1])
    mine = lax.dynamic_index_in_dim(split, core, 1, False)
    theirs = lax.dynamic_index_in_dim(split, 1 - core, 1, False)
    chip_sum = mine.astype(F32) + swap_core(theirs).astype(F32)
    home = lax.dynamic_index_in_dim(chip_sum, chip, 0, False)
    away = lax.dynamic_index_in_dim(chip_sum, 1 - chip, 0, False).astype(BF16)
    return home, away


def adamw_step(param, first, second, gradient, rate_value, decay_value):
    moment = 0.9 * first.astype(F32) + 0.1 * gradient
    variance = 0.999 * second + 0.001 * gradient * gradient
    update = (
        moment / (1.0 - 0.9**STEP) / (jnp.sqrt(variance / (1.0 - 0.999**STEP)) + 1e-08)
        + decay_value * param
    )
    return (param - rate_value * update, moment.astype(BF16), variance)


def per_device(
    tokens,
    labels,
    source,
    learn_rate,
    weight_decay,
    classifier,
    up_param,
    up_first,
    up_second,
    down_param,
    down_first,
    down_second,
):
    members = lax.axis_size("member")
    shards = lax.axis_size("dp")
    me = lax.axis_index("member")
    place = lax.axis_index("dp")
    chip, core = place // 2, place % 2
    tokens, labels = tokens[0], labels[0]
    up_param, up_first, up_second = up_param[0], up_first[0], up_second[0]
    down_param, down_first, down_second = down_param[0], down_first[0], down_second[0]
    direct = members == DIRECT_MEMBERS
    plan = find_plan(source, me) if direct else None
    loses = plan[-1] if direct else source[me] != me

    def begin(upper, lower):
        return exchange_start(upper, lower, plan, members) if direct else ()

    def finish(upper, lower, halves):
        if direct:
            return exchange_finish(upper, lower, halves, plan, members)
        return take_through_all(upper, source, members), take_through_all(lower, source, members)

    up_own, down_own = up_param.astype(BF16), wide(down_param.astype(BF16))
    up_taken, down_taken = finish(up_own, down_own, begin(up_own, down_own))
    up_short = jnp.where(loses, up_taken, up_own)
    down_short = jnp.where(loses, down_taken, down_own)
    both = jnp.stack([up_short, down_short])
    far = swap_chip(both)
    near = swap_core(both)
    up_state = jnp.stack([up_first, up_second.astype(BF16)])
    down_state = jnp.stack([wide(down_first), wide(down_second.astype(BF16))])
    up_state, down_state = after((up_state, down_state), both)
    state_halves = begin(up_state, down_state)
    far, _ = lax.optimization_barrier((far, state_halves))
    diagonal = swap_core(far)
    up_full = place_rows(both[0], near[0], far[0], diagonal[0], place)
    down_full = place_rows(*(narrow(block[1]) for block in (both, near, far, diagonal)), place)

    images, patches, features = tokens.shape
    hidden_units = up_full.shape[1]
    batch_total = images * shards
    padded = -(-patches // 16) * 16
    token_rows = jnp.pad(tokens, ((0, 0), (0, padded - patches), (0, 0)))
    token_rows = token_rows.reshape(images * padded, features).astype(F32)
    center = token_rows - jnp.mean(token_rows, axis=1, keepdims=True)
    normed = (center * lax.rsqrt(jnp.mean(center * center, axis=1, keepdims=True) + 1e-06)).astype(BF16)
    preact = jnp.dot(normed, up_full, preferred_element_type=F32) * features ** (-0.5)
    activated = (0.5 * preact * (1.0 + lax.erf(preact * 0.7071067811865476))).astype(BF16)
    down_scale = hidden_units ** (-0.5)
    residual = token_rows + jnp.dot(activated, down_full, preferred_element_type=F32) * down_scale
    out_center = residual - jnp.mean(residual, axis=1, keepdims=True)
    inverse = lax.rsqrt(jnp.mean(out_center * out_center, axis=1, keepdims=True) + 1e-06)
    out_normed = out_center * inverse
    pooled = (jnp.sum(out_normed.reshape(images, padded, features), axis=1) / patches).astype(BF16)
    logits = jnp.dot(pooled, classifier, preferred_element_type=F32)
    powered = jnp.exp(logits)
    softmax_out = powered / jnp.sum(powered, axis=1, keepdims=True)
    onehot = (labels[:, None] == jnp.arange(classifier.shape[1], dtype=jnp.int32)[None, :]).astype(F32)
    logit_delta = ((softmax_out - onehot) / batch_total).astype(BF16)
    pool_delta = (
        lax.dot_general(logit_delta, classifier, (((1,), (1,)), ((), ())), preferred_element_type=F32)
        / patches
    )
    token_delta = jnp.broadcast_to(pool_delta[:, None, :], (images, padded, features)).reshape(
        images * padded, features
    )
    residual_delta = inverse * (
        token_delta
        - jnp.mean(token_delta, axis=1, keepdims=True)
        - out_normed * jnp.mean(token_delta * out_normed, axis=1, keepdims=True)
    )
    residual_delta = residual_delta.astype(BF16)
    down_gradient = (
        lax.dot_general(activated, residual_delta, (((0,), (0,)), ((), ())), preferred_element_type=F32)
        * down_scale
    ).astype(BF16)
    down_home, down_away = sum_in_chip(down_gradient, chip, core)
    down_share = down_home + swap_chip(down_away).astype(F32)
    hidden_delta = (
        lax.dot_general(residual_delta, down_full, (((1,), (1,)), ((), ())), preferred_element_type=F32)
        * down_scale
    )
    derivative = (
        0.5 * (1.0 + lax.erf(preact * 0.7071067811865476))
        + preact * jnp.exp(-0.5 * preact * preact) * 0.3989422804014327
    )
    preact_delta = (hidden_delta * derivative).astype(BF16)
    up_gradient = (
        lax.dot_general(normed, preact_delta, (((0,), (0,)), ((), ())), preferred_element_type=F32)
        * features ** (-0.5)
    ).astype(BF16)
    up_home, up_away = sum_in_chip(up_gradient, chip, core)
    up_share = up_home + swap_chip(up_away).astype(F32)
    up_state, down_state = after((up_state, down_state), (up_away, down_away))
    up_state, down_state = finish(up_state, down_state, state_halves)

    def kept(own, short):
        return jnp.where(loses, short.astype(own.dtype), own)

    rate_value = learn_rate[0]
    decay_value = weight_decay[0]
    up_new = adamw_step(
        kept(up_param, up_taken),
        kept(up_first, up_state[0]),
        kept(up_second, up_state[1]),
        up_share,
        rate_value,
        decay_value,
    )
    down_new = adamw_step(
        kept(down_param, narrow(down_taken)),
        kept(down_first, narrow(down_state[0])),
        kept(down_second, narrow(down_state[1])),
        down_share,
        rate_value,
        decay_value,
    )
    return tuple(part[None] for part in up_new + down_new)


def solution(mesh):
    rows = P("member", "dp", None)
    placed = (
        P("member", "dp", None, None),
        P("member", "dp"),
        P(),
        P("member"),
        P("member"),
        P(),
        rows,
        rows,
        rows,
        rows,
        rows,
        rows,
    )
    return jax.shard_map(per_device, mesh=mesh, in_specs=placed, out_specs=(rows,) * 6, check_vma=False)
```

```python
import jax
import jax.numpy as jnp
from jax import lax
from jax.experimental import pallas as pl
from jax.experimental.pallas import tpu as pltpu
from jax.sharding import PartitionSpec as P

STEP = 1000
DIRECT_MEMBERS = 8
F32 = jnp.float32
BF16 = jnp.bfloat16


def after(value, token):
    return lax.optimization_barrier((value, token))[0]


def pairs_of(members):
    return [(one, two) for one in range(members) for two in range(one + 1, members)]


def plan_kernel(members, source_ref, me_ref, first, second, third, fourth, shared, is_one, loses):
    none = members * (members - 1) // 2

    def place_of(one, two):
        low, high = jnp.minimum(one, two), jnp.maximum(one, two)
        return jnp.right_shift(low * (2 * members - 1 - low), 1) + high - low - 1

    zero = jnp.int32(0)
    taker_one = taker_two = source_one = source_two = zero
    for index in range(members):
        own = source_ref[index]
        takes = own != index
        taker_two = jnp.where(takes, index, taker_two)
        source_two = jnp.where(takes, own, source_two)
        back = members - 1 - index
        own = source_ref[back]
        takes = own != back
        taker_one = jnp.where(takes, back, taker_one)
        source_one = jnp.where(takes, own, source_one)
    same = source_one == source_two
    first[0] = place_of(source_one, taker_one)
    second[0] = place_of(source_two, taker_two)
    third[0] = jnp.where(same, place_of(taker_one, taker_two), place_of(source_one, taker_one))
    fourth[0] = jnp.where(same, none, place_of(source_two, taker_two))
    shared[0] = jnp.where(same, 1, 0)
    me = me_ref[0]
    is_one[0] = jnp.where(me == taker_one, 1, 0)
    loses[0] = jnp.where((me == taker_one) | (me == taker_two), 1, 0)


def find_plan(source, me):
    members = source.shape[0]
    scalars = pl.pallas_call(
        lambda *refs: plan_kernel(members, *refs),
        out_shape=[jax.ShapeDtypeStruct((1,), jnp.int32)] * 7,
        in_specs=[pl.BlockSpec(memory_space=pltpu.SMEM)] * 2,
        out_specs=[pl.BlockSpec(memory_space=pltpu.SMEM)] * 7,
    )(source, me.reshape(1))
    first, second, third, fourth, shared, is_one, loses = (scalar.reshape(()) for scalar in scalars)
    return first, second, third, fourth, shared == 1, is_one == 1, loses == 1


def swap_pair(value, place, members):
    def branch(one, two):
        return lambda part: lax.ppermute(part, "member", [(one, two), (two, one)])

    return lax.switch(place, [branch(one, two) for one, two in pairs_of(members)] + [lambda part: part], value)


def exchange_start(upper, lower, plan, members):
    first, second, _, _, shared = plan[:5]
    to_one = swap_pair(upper, first, members)
    to_two = swap_pair(after(jnp.where(shared, lower, upper), to_one), second, members)
    return to_one, to_two


def exchange_finish(upper, lower, halves, plan, members):
    to_one, to_two = halves
    _, _, third, fourth, shared, is_one, _ = plan
    to_third = swap_pair(jnp.where(shared, jnp.where(is_one, to_one, to_two), lower), third, members)
    to_fourth = swap_pair(after(lower, to_third), fourth, members)
    return (
        jnp.where(is_one, to_one, jnp.where(shared, to_third, to_two)),
        jnp.where(is_one, to_third, jnp.where(shared, to_two, to_fourth)),
    )


def wide(value):
    half = value.shape[0] // 2
    return jnp.concatenate([value[:half], value[half:]], axis=1)


def narrow(value):
    half = value.shape[1] // 2
    return jnp.concatenate([value[:, :half], value[:, half:]], axis=0)


def take_through_all(value, source, members):
    flat = value.reshape(members, -1)
    parts = lax.all_to_all(flat, "member", split_axis=0, concat_axis=0, tiled=True)
    picked = jnp.take(parts, source, axis=0)
    return lax.all_to_all(picked, "member", split_axis=0, concat_axis=0, tiled=True).reshape(value.shape)


def swap_core(value):
    return lax.ppermute(value, "dp", [(0, 1), (1, 0), (2, 3), (3, 2)])


def swap_chip(value):
    return lax.ppermute(value, "dp", [(0, 2), (2, 0), (1, 3), (3, 1)])


TILE = 256
ROWS = 16


def gradient_kernel(
    images,
    patches,
    batch_total,
    place_ref,
    label_ref,
    tokens_ref,
    classifier_ref,
    own_ref,
    near_ref,
    far_ref,
    diagonal_ref,
    own_out,
    near_out,
    far_out,
    diagonal_out,
    up_ref,
    down_ref,
    classes_ref,
    normed_ref,
    active_ref,
    slope_ref,
    residual_ref,
    inverse_ref,
    pooled_ref,
    delta_ref,
    up_grad_ref,
    down_grad_ref,
):
    rows, features = tokens_ref.shape
    hidden = up_ref.shape[1]
    share = own_ref.shape[1]
    per_image = rows // images
    place = place_ref[0]
    up_scale = features ** (-0.5)
    down_scale = hidden ** (-0.5)

    for step, block in enumerate((own_ref, near_ref, far_ref, diagonal_ref)):
        at = pl.multiple_of((place ^ step) * share, share)
        up_ref[pl.ds(at, share), :] = block[0]
        at = pl.multiple_of((place ^ step) * (2 * share), 2 * share)
        down_ref[pl.ds(at, share), :] = block[1, :, :features]
        down_ref[pl.ds(at + share, share), :] = block[1, :, features:]
    classes = classifier_ref.shape[1]
    classes_ref[...] = jnp.zeros_like(classes_ref)
    classes_ref[:, :classes] = classifier_ref[...]

    def norm_rows(step, carry):
        here = pl.ds(pl.multiple_of(step * ROWS, ROWS), ROWS)
        value = tokens_ref[here, :].astype(F32)
        center = value - jnp.mean(value, axis=1, keepdims=True)
        spread = jnp.mean(center * center, axis=1, keepdims=True)
        normed_ref[here, :] = (center * lax.rsqrt(spread + 1e-06)).astype(BF16)
        return carry

    lax.fori_loop(0, rows // ROWS, norm_rows, 0, unroll=4)

    def up_tile(step, carry):
        here = pl.ds(pl.multiple_of(step * TILE, TILE), TILE)
        preact = jnp.dot(normed_ref[...], up_ref[:, here], preferred_element_type=F32) * up_scale
        half = 0.5 * (1.0 + lax.erf(preact * 0.7071067811865476))
        active_ref[:, here] = (preact * half).astype(BF16)
        slope_ref[:, here] = half + preact * jnp.exp(-0.5 * preact * preact) * 0.3989422804014327
        return carry

    lax.fori_loop(0, hidden // TILE, up_tile, 0)

    def down_tile(step, carry):
        here = pl.ds(pl.multiple_of(step * TILE, TILE), TILE)
        product = jnp.dot(active_ref[...], down_ref[:, here], preferred_element_type=F32)
        residual_ref[:, here] = tokens_ref[:, here].astype(F32) + product * down_scale
        return carry

    lax.fori_loop(0, features // TILE, down_tile, 0)

    def norm_out(step, total):
        here = pl.ds(pl.multiple_of(step * ROWS, ROWS), ROWS)
        value = residual_ref[here, :]
        center = value - jnp.mean(value, axis=1, keepdims=True)
        spread = jnp.mean(center * center, axis=1, keepdims=True)
        inverse = lax.rsqrt(spread + 1e-06)
        out = center * inverse
        residual_ref[here, :] = out
        inverse_ref[here, :] = jnp.broadcast_to(inverse, (ROWS, inverse_ref.shape[1]))
        return total + out[:8] + out[8:]

    blocks = per_image // ROWS
    pooled_ref[...] = jnp.zeros_like(pooled_ref)
    for image in range(images):
        total = lax.fori_loop(
            image * blocks, (image + 1) * blocks, norm_out, jnp.zeros((8, features), F32), unroll=blocks
        )
        pooled_ref[pl.ds(image, 1), :] = jnp.sum(total, axis=0, keepdims=True) * (1.0 / patches)

    logits = jnp.dot(pooled_ref[...].astype(BF16), classes_ref[...], preferred_element_type=F32)
    kind = lax.broadcasted_iota(jnp.int32, logits.shape, 1)
    image_row = lax.broadcasted_iota(jnp.int32, logits.shape, 0)
    powered = jnp.where(kind < classes, jnp.exp(logits), 0.0)
    softmax_out = powered / jnp.sum(powered, axis=1, keepdims=True)
    label = jnp.full(logits.shape, -1, jnp.int32)
    for image in range(images):
        label = jnp.where(image_row == image, label_ref[image], label)
    onehot = jnp.where(kind == label, 1.0, 0.0)
    logit_delta = ((softmax_out - onehot) * (1.0 / batch_total)).astype(BF16)
    pool_delta = lax.dot_general(
        logit_delta, classes_ref[...], (((1,), (1,)), ((), ())), preferred_element_type=F32
    ) * (1.0 / patches)
    pool_center = pool_delta - jnp.mean(pool_delta, axis=1, keepdims=True)

    for image in range(images):
        token_delta = pool_delta[image : image + 1]
        token_center = pool_center[image : image + 1]

        def delta_rows(step, carry):
            here = pl.ds(pl.multiple_of(step * ROWS, ROWS), ROWS)
            out = residual_ref[here, :]
            along = jnp.mean(token_delta * out, axis=1, keepdims=True)
            inverse = inverse_ref[here, :][:, :1]
            delta_ref[here, :] = (inverse * (token_center - out * along)).astype(BF16)
            return carry

        lax.fori_loop(image * blocks, (image + 1) * blocks, delta_rows, 0, unroll=blocks)

    def back_tile(step, carry):
        here = pl.ds(pl.multiple_of(step * TILE, TILE), TILE)
        down_grad_ref[here, :] = (
            lax.dot_general(
                active_ref[:, here], delta_ref[...], (((0,), (0,)), ((), ())), preferred_element_type=F32
            )
            * down_scale
        ).astype(BF16)
        hidden_delta = lax.dot_general(
            delta_ref[...], down_ref[here, :], (((1,), (1,)), ((), ())), preferred_element_type=F32
        )
        preact_delta = (hidden_delta * down_scale * slope_ref[:, here]).astype(BF16)
        up_grad_ref[:, here] = (
            lax.dot_general(
                normed_ref[...], preact_delta, (((0,), (0,)), ((), ())), preferred_element_type=F32
            )
            * up_scale
        ).astype(BF16)
        return carry

    lax.fori_loop(0, hidden // TILE, back_tile, 0)

    for step, block in enumerate((own_out, near_out, far_out, diagonal_out)):
        at = pl.multiple_of((place ^ step) * share, share)
        block[0] = up_grad_ref[pl.ds(at, share), :]
        at = pl.multiple_of((place ^ step) * (2 * share), 2 * share)
        block[1, :, :features] = down_grad_ref[pl.ds(at, share), :]
        block[1, :, features:] = down_grad_ref[pl.ds(at + share, share), :]


def gradients(tokens, labels, place, shards, classifier, blocks):
    images, patches, features = tokens.shape
    share, hidden = blocks[0].shape[1:]
    padded = -(-patches // ROWS) * ROWS
    rows = images * padded
    tokens = jnp.pad(tokens, ((0, 0), (0, padded - patches), (0, 0))).reshape(rows, features)
    in_smem = pl.BlockSpec(memory_space=pltpu.SMEM)
    in_vmem = pl.BlockSpec(memory_space=pltpu.VMEM)
    width = -(-classifier.shape[1] // 128) * 128
    return pl.pallas_call(
        lambda *refs: gradient_kernel(images, patches, images * shards, *refs),
        out_shape=[jax.ShapeDtypeStruct(blocks[0].shape, BF16)] * 4,
        in_specs=[in_smem] * 2 + [in_vmem] * 6,
        out_specs=[in_vmem] * 4,
        scratch_shapes=[
            pltpu.VMEM((features, hidden), BF16),
            pltpu.VMEM((hidden, features), BF16),
            pltpu.VMEM((features, width), BF16),
            pltpu.VMEM((rows, features), BF16),
            pltpu.VMEM((rows, hidden), BF16),
            pltpu.VMEM((rows, hidden), F32),
            pltpu.VMEM((rows, features), F32),
            pltpu.VMEM((rows, 128), F32),
            pltpu.VMEM((8, features), F32),
            pltpu.VMEM((rows, features), BF16),
            pltpu.VMEM((features, hidden), BF16),
            pltpu.VMEM((hidden, features), BF16),
        ],
        compiler_params=pltpu.CompilerParams(vmem_limit_bytes=56 * 1024 * 1024),
        cost_estimate=pl.CostEstimate(flops=10 * rows * features * hidden, bytes_accessed=12 * 1024 * 1024, transcendentals=0),
    )(place.reshape(1), labels, tokens, classifier, *blocks)


def adamw_step(param, first, second, gradient, rate_value, decay_value):
    moment = 0.9 * first.astype(F32) + 0.1 * gradient
    variance = 0.999 * second + 0.001 * gradient * gradient
    update = (
        moment / (1.0 - 0.9**STEP) / (jnp.sqrt(variance / (1.0 - 0.999**STEP)) + 1e-08)
        + decay_value * param
    )
    return (param - rate_value * update, moment.astype(BF16), variance)


def per_device(
    tokens,
    labels,
    source,
    learn_rate,
    weight_decay,
    classifier,
    up_param,
    up_first,
    up_second,
    down_param,
    down_first,
    down_second,
):
    members = lax.axis_size("member")
    me = lax.axis_index("member")
    place = lax.axis_index("dp")
    tokens, labels = tokens[0], labels[0]
    up_param, up_first, up_second = up_param[0], up_first[0], up_second[0]
    down_param, down_first, down_second = down_param[0], down_first[0], down_second[0]
    direct = members == DIRECT_MEMBERS
    plan = find_plan(source, me) if direct else None
    loses = plan[-1] if direct else source[me] != me

    def begin(upper, lower):
        return exchange_start(upper, lower, plan, members) if direct else ()

    def finish(upper, lower, halves):
        if direct:
            return exchange_finish(upper, lower, halves, plan, members)
        return take_through_all(upper, source, members), take_through_all(lower, source, members)

    up_own, down_own = up_param.astype(BF16), wide(down_param.astype(BF16))
    up_taken, down_taken = finish(up_own, down_own, begin(up_own, down_own))
    up_short = jnp.where(loses, up_taken, up_own)
    down_short = jnp.where(loses, down_taken, down_own)
    both = jnp.stack([up_short, down_short])
    far = swap_chip(both)
    near = swap_core(both)
    up_state = jnp.stack([up_first, up_second.astype(BF16)])
    down_state = jnp.stack([wide(down_first), wide(down_second.astype(BF16))])
    up_state, down_state = after((up_state, down_state), both)
    state_halves = begin(up_state, down_state)
    far, _ = lax.optimization_barrier((far, state_halves))
    diagonal = swap_core(far)
    own_terms, near_terms, far_terms, diagonal_terms = gradients(
        tokens, labels, place, lax.axis_size("dp"), classifier, (both, near, far, diagonal)
    )
    from_near = swap_core(near_terms)
    from_diagonal = swap_core(diagonal_terms)
    away = (far_terms.astype(F32) + from_diagonal.astype(F32)).astype(BF16)
    shares = own_terms.astype(F32) + from_near.astype(F32) + swap_chip(away).astype(F32)
    up_share, down_share = shares[0], narrow(shares[1])
    up_state, down_state = after((up_state, down_state), away)
    up_state, down_state = finish(up_state, down_state, state_halves)

    def kept(own, short):
        return jnp.where(loses, short.astype(own.dtype), own)

    rate_value = learn_rate[0]
    decay_value = weight_decay[0]
    up_new = adamw_step(
        kept(up_param, up_taken),
        kept(up_first, up_state[0]),
        kept(up_second, up_state[1]),
        up_share,
        rate_value,
        decay_value,
    )
    down_new = adamw_step(
        kept(down_param, narrow(down_taken)),
        kept(down_first, narrow(down_state[0])),
        kept(down_second, narrow(down_state[1])),
        down_share,
        rate_value,
        decay_value,
    )
    return tuple(part[None] for part in up_new + down_new)


def solution(mesh):
    rows = P("member", "dp", None)
    placed = (
        P("member", "dp", None, None),
        P("member", "dp"),
        P(),
        P("member"),
        P("member"),
        P(),
        rows,
        rows,
        rows,
        rows,
        rows,
        rows,
    )
    return jax.shard_map(per_device, mesh=mesh, in_specs=placed, out_specs=(rows,) * 6, check_vma=False)
```

```python
import jax
import jax.numpy as jnp
from jax import lax
from jax.experimental import pallas as pl
from jax.experimental.pallas import tpu as pltpu
from jax.sharding import PartitionSpec as P

STEP = 1000
DIRECT_MEMBERS = 8
F32 = jnp.float32
BF16 = jnp.bfloat16


def after(value, token):
    return lax.optimization_barrier((value, token))[0]


def pairs_of(members):
    return [(one, two) for one in range(members) for two in range(one + 1, members)]


def plan_kernel(members, source_ref, me_ref, first, second, third, fourth, shared, is_one, loses, choices):
    none = members * (members - 1) // 2

    def place_of(one, two):
        low, high = jnp.minimum(one, two), jnp.maximum(one, two)
        return jnp.right_shift(low * (2 * members - 1 - low), 1) + high - low - 1

    zero = jnp.int32(0)
    taker_one = taker_two = source_one = source_two = zero
    for index in range(members):
        own = source_ref[index]
        takes = own != index
        taker_two = jnp.where(takes, index, taker_two)
        source_two = jnp.where(takes, own, source_two)
        back = members - 1 - index
        own = source_ref[back]
        takes = own != back
        taker_one = jnp.where(takes, back, taker_one)
        source_one = jnp.where(takes, own, source_one)
    same = source_one == source_two
    first[0] = place_of(source_one, taker_one)
    second[0] = place_of(source_two, taker_two)
    third[0] = jnp.where(same, place_of(taker_one, taker_two), place_of(source_one, taker_one))
    fourth[0] = jnp.where(same, none, place_of(source_two, taker_two))
    shared[0] = jnp.where(same, 1, 0)
    me = me_ref[0]
    is_one[0] = jnp.where(me == taker_one, 1, 0)
    loses[0] = jnp.where((me == taker_one) | (me == taker_two), 1, 0)
    two_or = jnp.where(me == taker_two, jnp.where(same, 3, 2), 0)
    choices[0] = jnp.where(me == taker_one, 1, two_or)
    two_or = jnp.where(me == taker_two, jnp.where(same, 2, 3), 0)
    choices[1] = jnp.where(me == taker_one, 1, two_or)


def find_plan(source, me):
    members = source.shape[0]
    scalars = pl.pallas_call(
        lambda *refs: plan_kernel(members, *refs),
        out_shape=[jax.ShapeDtypeStruct((1,), jnp.int32)] * 7 + [jax.ShapeDtypeStruct((2,), jnp.int32)],
        in_specs=[pl.BlockSpec(memory_space=pltpu.SMEM)] * 2,
        out_specs=[pl.BlockSpec(memory_space=pltpu.SMEM)] * 8,
    )(source, me.reshape(1))
    first, second, third, fourth, shared, is_one, loses = (scalar.reshape(()) for scalar in scalars[:7])
    return first, second, third, fourth, shared == 1, is_one == 1, loses == 1, scalars[7]


def swap_pair(value, place, members):
    def branch(one, two):
        return lambda part: lax.ppermute(part, "member", [(one, two), (two, one)])

    return lax.switch(place, [branch(one, two) for one, two in pairs_of(members)] + [lambda part: part], value)


def exchange_start(upper, lower, plan, members):
    first, second, _, _, shared = plan[:5]
    to_one = swap_pair(upper, first, members)
    to_two = swap_pair(after(jnp.where(shared, lower, upper), to_one), second, members)
    return to_one, to_two


def exchange_finish(upper, lower, halves, plan, members):
    to_one, to_two = halves
    third, fourth, shared, is_one = plan[2:6]
    to_third = swap_pair(jnp.where(shared, jnp.where(is_one, to_one, to_two), lower), third, members)
    to_fourth = swap_pair(after(lower, to_third), fourth, members)
    return to_third, to_fourth


def wide(value):
    half = value.shape[0] // 2
    return jnp.concatenate([value[:half], value[half:]], axis=1)


def take_through_all(value, source, members):
    flat = value.reshape(members, -1)
    parts = lax.all_to_all(flat, "member", split_axis=0, concat_axis=0, tiled=True)
    picked = jnp.take(parts, source, axis=0)
    return lax.all_to_all(picked, "member", split_axis=0, concat_axis=0, tiled=True).reshape(value.shape)


def swap_core(value):
    return lax.ppermute(value, "dp", [(0, 1), (1, 0), (2, 3), (3, 2)])


def swap_chip(value):
    return lax.ppermute(value, "dp", [(0, 2), (2, 0), (1, 3), (3, 1)])


TILE = 512
ROWS = 16


def gradient_kernel(
    images,
    patches,
    batch_total,
    place_ref,
    label_ref,
    tokens_hbm,
    classifier_hbm,
    up_own,
    up_near,
    up_far,
    up_diagonal,
    down_own,
    down_near,
    down_far,
    down_diagonal,
    own_out,
    near_out,
    far_out,
    diagonal_out,
    tokens_ref,
    classifier_ref,
    up_ref,
    down_ref,
    classes_ref,
    normed_ref,
    turned_ref,
    active_ref,
    slope_ref,
    residual_ref,
    inverse_ref,
    delta_ref,
    up_grad_ref,
    down_grad_ref,
    arrived,
    left,
):
    rows, features = residual_ref.shape
    hidden = up_ref.shape[1]
    share = up_own.shape[0]
    place = place_ref[0]
    up_scale = features ** (-0.5)
    down_scale = hidden ** (-0.5)

    tokens_copy = pltpu.make_async_copy(tokens_hbm, tokens_ref, arrived.at[12])
    classifier_copy = pltpu.make_async_copy(classifier_hbm, classifier_ref, arrived.at[13])
    tokens_copy.start()
    residual_ref[pl.ds(images * patches, rows - images * patches), :] = jnp.zeros(
        (rows - images * patches, features), F32
    )
    up_copies, down_copies = [], []
    for step, block in enumerate((up_own, up_near, up_far, up_diagonal)):
        at = pl.multiple_of((place ^ step) * share, share)
        up_copies.append(pltpu.make_async_copy(block, up_ref.at[pl.ds(at, share), :], arrived.at[step]))
    for step, block in enumerate((down_own, down_near, down_far, down_diagonal)):
        for half in range(2):
            at = pl.multiple_of((place ^ step) * (2 * share) + half * share, share)
            down_copies.append(
                pltpu.make_async_copy(
                    block.at[:, pl.ds(half * features, features)],
                    down_ref.at[pl.ds(at, share), :],
                    arrived.at[4 + 2 * step + half],
                )
            )
    for copy in up_copies + down_copies + [classifier_copy]:
        copy.start()

    tokens_copy.wait()
    for step in range(patches):
        residual_ref[pl.ds(step * images, images), :] = tokens_ref[step].astype(F32)

    def norm_rows(step, carry):
        here = pl.ds(pl.multiple_of(step * ROWS, ROWS), ROWS)
        value = residual_ref[here, :]
        center = value - jnp.mean(value, axis=1, keepdims=True)
        spread = jnp.mean(center * center, axis=1, keepdims=True)
        normed_ref[here, :] = (center * lax.rsqrt(spread + 1e-06)).astype(BF16)
        return carry

    lax.fori_loop(0, rows // ROWS, norm_rows, 0, unroll=True)
    turned_ref[...] = normed_ref[...].T
    for copy in up_copies:
        copy.wait()

    def up_tile(step, carry):
        here = pl.ds(pl.multiple_of(step * TILE, TILE), TILE)
        preact = jnp.dot(normed_ref[...], up_ref[:, here], preferred_element_type=F32) * up_scale
        half = 0.5 * (1.0 + lax.erf(preact * 0.7071067811865476))
        active_ref[:, here] = (preact * half).astype(BF16)
        slope_ref[:, here] = half + preact * jnp.exp(-0.5 * preact * preact) * 0.3989422804014327
        return carry

    lax.fori_loop(0, hidden // TILE, up_tile, 0, unroll=3)
    for copy in down_copies:
        copy.wait()

    product = jnp.dot(active_ref[...], down_ref[...], preferred_element_type=F32)
    residual_ref[...] += product * down_scale

    def norm_out(step, total):
        here = pl.ds(pl.multiple_of(step * ROWS, ROWS), ROWS)
        value = residual_ref[here, :]
        center = value - jnp.mean(value, axis=1, keepdims=True)
        spread = jnp.mean(center * center, axis=1, keepdims=True)
        inverse = lax.rsqrt(spread + 1e-06)
        out = center * inverse
        residual_ref[here, :] = out
        inverse_ref[here, :] = jnp.broadcast_to(inverse, (ROWS, inverse_ref.shape[1]))
        return total + out[:8] + out[8:]

    total = lax.fori_loop(0, rows // ROWS, norm_out, jnp.zeros((8, features), F32), unroll=True)
    fold = images
    while fold < 8:
        total = total + jnp.concatenate([total[fold:], total[:fold]], axis=0)
        fold *= 2
    pooled = (total * (1.0 / patches)).astype(BF16)
    classifier_copy.wait()
    classes = classifier_ref.shape[0]
    classes_ref[...] = jnp.zeros_like(classes_ref)
    classes_ref[:classes, :] = classifier_ref[...].astype(F32)
    heads = classes_ref[...].astype(BF16)
    logits = lax.dot_general(pooled, heads, (((1,), (1,)), ((), ())), preferred_element_type=F32)
    kind = lax.broadcasted_iota(jnp.int32, logits.shape, 1)
    image_row = lax.broadcasted_iota(jnp.int32, logits.shape, 0)
    powered = jnp.where(kind < classes, jnp.exp(logits), 0.0)
    softmax_out = powered / jnp.sum(powered, axis=1, keepdims=True)
    label = jnp.full(logits.shape, -1, jnp.int32)
    for image in range(images):
        label = jnp.where(image_row % images == image, label_ref[image], label)
    onehot = jnp.where(kind == label, 1.0, 0.0)
    logit_delta = ((softmax_out - onehot) * (1.0 / batch_total)).astype(BF16)
    pool_delta = jnp.dot(logit_delta, heads, preferred_element_type=F32) * (1.0 / patches)
    pool_center = pool_delta - jnp.mean(pool_delta, axis=1, keepdims=True)

    token_delta = jnp.concatenate([pool_delta, pool_delta], axis=0)
    token_center = jnp.concatenate([pool_center, pool_center], axis=0)

    def delta_rows(step, carry):
        here = pl.ds(pl.multiple_of(step * ROWS, ROWS), ROWS)
        out = residual_ref[here, :]
        along = jnp.mean(token_delta * out, axis=1, keepdims=True)
        inverse = inverse_ref[here, :][:, :1]
        delta_ref[here, :] = (inverse * (token_center - out * along)).astype(BF16)
        return carry

    lax.fori_loop(0, rows // ROWS, delta_rows, 0, unroll=True)

    def back_tile(step, carry):
        here = pl.ds(pl.multiple_of(step * TILE, TILE), TILE)
        down_grad_ref[here, :] = (
            lax.dot_general(
                active_ref[:, here], delta_ref[...], (((0,), (0,)), ((), ())), preferred_element_type=F32
            )
            * down_scale
        ).astype(BF16)
        hidden_delta = lax.dot_general(
            delta_ref[...], down_ref[here, :], (((1,), (1,)), ((), ())), preferred_element_type=F32
        )
        preact_delta = (hidden_delta * down_scale * slope_ref[:, here]).astype(BF16)
        active_ref[:, here] = preact_delta
        return carry

    lax.fori_loop(0, hidden // TILE, back_tile, 0, unroll=3)

    outputs = (own_out, near_out, far_out, diagonal_out)
    leaving = []
    for step, block in enumerate(outputs):
        for half in range(2):
            at = pl.multiple_of((place ^ step) * (2 * share) + half * share, share)
            leaving.append(
                pltpu.make_async_copy(
                    down_grad_ref.at[pl.ds(at, share), :],
                    block.at[1, :, pl.ds(half * features, features)],
                    left.at[len(leaving)],
                )
            )
            leaving[-1].start()
    for tile in range(hidden // TILE):
        here = pl.ds(tile * TILE, TILE)
        up_grad_ref[:, here] = (
            jnp.dot(turned_ref[...], active_ref[:, here], preferred_element_type=F32) * up_scale
        ).astype(BF16)
        for step, block in enumerate(outputs):
            at = pl.multiple_of((place ^ step) * share, share)
            leaving.append(
                pltpu.make_async_copy(
                    up_grad_ref.at[pl.ds(at, share), here], block.at[0, :, here], left.at[len(leaving)]
                )
            )
            leaving[-1].start()
    for copy in leaving:
        copy.wait()


def gradients(tokens, labels, place, shards, classifier, up_blocks, down_blocks):
    images, patches, features = tokens.shape
    share, hidden = up_blocks[0].shape
    rows = -(-images * patches // 64) * 64
    tokens = tokens.transpose(1, 0, 2)
    classifier = classifier.T
    in_smem = pl.BlockSpec(memory_space=pltpu.SMEM)
    anywhere = pl.BlockSpec(memory_space=pltpu.HBM)
    width = -(-classifier.shape[0] // 128) * 128
    return pl.pallas_call(
        lambda *refs: gradient_kernel(images, patches, images * shards, *refs),
        out_shape=[jax.ShapeDtypeStruct((2, share, hidden), BF16)] * 4,
        in_specs=[in_smem] * 2 + [anywhere] * 10,
        out_specs=[anywhere] * 4,
        scratch_shapes=[
            pltpu.VMEM(tokens.shape, BF16),
            pltpu.VMEM(classifier.shape, BF16),
            pltpu.VMEM((features, hidden), BF16),
            pltpu.VMEM((hidden, features), BF16),
            pltpu.VMEM((width, features), F32),
            pltpu.VMEM((rows, features), BF16),
            pltpu.VMEM((features, rows), BF16),
            pltpu.VMEM((rows, hidden), BF16),
            pltpu.VMEM((rows, hidden), F32),
            pltpu.VMEM((rows, features), F32),
            pltpu.VMEM((rows, 128), F32),
            pltpu.VMEM((rows, features), BF16),
            pltpu.VMEM((features, hidden), BF16),
            pltpu.VMEM((hidden, features), BF16),
            pltpu.SemaphoreType.DMA((14,)),
            pltpu.SemaphoreType.DMA((8 + 4 * (hidden // TILE),)),
        ],
        compiler_params=pltpu.CompilerParams(vmem_limit_bytes=56 * 1024 * 1024),
        cost_estimate=pl.CostEstimate(
            flops=10 * rows * features * hidden, bytes_accessed=12 * 1024 * 1024, transcendentals=0
        ),
    )(place.reshape(1), labels, tokens, classifier, *up_blocks, *down_blocks)


CHUNKS = 4


def adamw_kernel(candidates, choice_ref, rate_ref, decay_ref, *refs):
    near, away, own = refs[:3]
    sides = []
    at = 3
    for _ in range(2):
        sides.append(refs[at : at + 4 + candidates])
        at += 4 + candidates
    outputs = refs[at : at + 6]
    buffers = refs[at + 6 : -2]
    arrived, left = refs[-2:]

    def spots(kind, chunk):
        rows, columns = sides[kind][0].shape
        step = rows // CHUNKS
        here = (pl.ds(chunk * step, step), slice(None))
        if not kind:
            return here, here
        half, part = divmod(chunk, CHUNKS // 2)
        return here, (pl.ds(part * step, step), pl.ds(half * columns, columns))

    def copies(kind, chunk):
        param, first, second, short = sides[kind][:4]
        taken = sides[kind][4:]
        here, there = spots(kind, chunk)
        held = buffers[9 * kind : 9 * kind + 9]
        old, old_short, moment, variance, variance_short, terms_own, terms_near, terms_away = (
            buffer.at[here] for buffer in held[:8]
        )
        base = (kind * CHUNKS + chunk) * 6

        def copy(source, target, index):
            return pltpu.make_async_copy(source, target, arrived.at[base + index])

        fixed = [
            copy(own.at[(kind,) + there], terms_own, 3),
            copy(near.at[(kind,) + there], terms_near, 4),
            copy(away.at[(kind,) + there], terms_away, 5),
        ]
        kept = [copy(param.at[here], old, 0), copy(first.at[here], moment, 1), copy(second.at[here], variance, 2)]

        def moved(index):
            return [
                copy(short.at[there], old_short, 0),
                copy(taken[index].at[(0,) + there], moment, 1),
                copy(taken[index].at[(1,) + there], variance_short, 2),
            ]

        return fixed, kept, moved

    choices = [choice_ref[0], choice_ref[1]]
    work = [(kind, chunk) for kind in range(2) for chunk in range(CHUNKS)]
    for kind, chunk in work:
        fixed, kept, moved = copies(kind, chunk)

        @pl.when(choices[kind] == 0)
        def _():
            for copy in kept:
                copy.start()

        for index in range(candidates):

            @pl.when(choices[kind] == index + 1)
            def _():
                for copy in moved(index):
                    copy.start()

        for copy in fixed:
            copy.start()

    rate, decay = rate_ref[0], decay_ref[0]
    leaving = []
    for kind, chunk in work:
        fixed, kept, moved = copies(kind, chunk)

        @pl.when(choices[kind] == 0)
        def _():
            for copy in kept:
                copy.wait()

        @pl.when(choices[kind] != 0)
        def _():
            for copy in moved(0):
                copy.wait()

        for copy in fixed:
            copy.wait()
        here, _ = spots(kind, chunk)
        held = buffers[9 * kind : 9 * kind + 9]
        old, old_short, moment_in, variance_in, variance_short, terms_own, terms_near, terms_away, moment_out = held
        own_state = choices[kind] == 0
        before = jnp.where(own_state, old[here], old_short[here].astype(F32))
        variance = jnp.where(own_state, variance_in[here], variance_short[here].astype(F32))
        gradient = terms_own[here].astype(F32) + terms_near[here].astype(F32) + terms_away[here].astype(F32)
        moment = 0.9 * moment_in[here].astype(F32) + 0.1 * gradient
        variance = 0.999 * variance + 0.001 * gradient * gradient
        root = jnp.sqrt(variance * (1.0 / (1.0 - 0.999**STEP))) + 1e-08
        update = moment * (1.0 / (1.0 - 0.9**STEP)) / root + decay * before
        old[here] = before - rate * update
        moment_out[here] = moment.astype(BF16)
        variance_in[here] = variance
        for source, target in zip((old, moment_out, variance_in), outputs[3 * kind : 3 * kind + 3]):
            leaving.append(pltpu.make_async_copy(source.at[here], target.at[here], left.at[len(leaving)]))
            leaving[-1].start()
    for copy in leaving:
        copy.wait()


def adamw(choices, rate, decay, shares, sides):
    candidates = len(sides[0]) - 4
    in_smem = pl.BlockSpec(memory_space=pltpu.SMEM)
    anywhere = pl.BlockSpec(memory_space=pltpu.HBM)
    outputs, buffers = [], []
    for side in sides:
        shape = side[0].shape
        outputs += [jax.ShapeDtypeStruct(shape, kind) for kind in (F32, BF16, F32)]
        buffers += [pltpu.VMEM(shape, kind) for kind in (F32, BF16, BF16, F32) + (BF16,) * 5]
    count = 2 * CHUNKS
    return pl.pallas_call(
        lambda *refs: adamw_kernel(candidates, *refs),
        out_shape=outputs,
        in_specs=[in_smem] * 3 + [anywhere] * (3 + 2 * (4 + candidates)),
        out_specs=[anywhere] * 6,
        scratch_shapes=buffers + [pltpu.SemaphoreType.DMA((6 * count,)), pltpu.SemaphoreType.DMA((3 * count,))],
        compiler_params=pltpu.CompilerParams(vmem_limit_bytes=56 * 1024 * 1024),
        cost_estimate=pl.CostEstimate(
            flops=40 * sides[0][0].size, bytes_accessed=16 * 1024 * 1024, transcendentals=0
        ),
    )(choices, rate, decay, *shares, *sides[0], *sides[1])


def per_device(
    tokens,
    labels,
    source,
    learn_rate,
    weight_decay,
    classifier,
    up_param,
    up_first,
    up_second,
    down_param,
    down_first,
    down_second,
):
    members = lax.axis_size("member")
    me = lax.axis_index("member")
    place = lax.axis_index("dp")
    tokens, labels = tokens[0], labels[0]
    up_param, up_first, up_second = up_param[0], up_first[0], up_second[0]
    down_param, down_first, down_second = down_param[0], down_first[0], down_second[0]
    up_own, down_own = up_param.astype(BF16), wide(down_param.astype(BF16))
    up_state = jnp.stack([up_first, up_second.astype(BF16)])
    down_state = jnp.stack([wide(down_first), wide(down_second.astype(BF16))])
    if members == DIRECT_MEMBERS:
        plan = find_plan(source, me)
        shared, is_one, loses, choices = plan[4:]
        to_one, to_two = halves = exchange_start(up_own, down_own, plan, members)
        to_third, to_fourth = exchange_finish(up_own, down_own, halves, plan, members)
        up_short = jnp.where(
            loses, jnp.where(is_one, to_one, jnp.where(shared, to_third, to_two)), up_own
        )
        down_short = jnp.where(
            loses, jnp.where(is_one, to_third, jnp.where(shared, to_two, to_fourth)), down_own
        )
    else:
        up_short = take_through_all(up_own, source, members)
        down_short = take_through_all(down_own, source, members)
        choices = jnp.where(source[me] != me, jnp.ones((2,), jnp.int32), 0)

    up_far, down_far = swap_chip(up_short), swap_chip(down_short)
    up_near, down_near = swap_core(up_short), swap_core(down_short)
    up_state, down_state = after((up_state, down_state), (up_short, down_short))
    if members == DIRECT_MEMBERS:
        halves = exchange_start(up_state, down_state, plan, members)
        up_far, down_far = after((up_far, down_far), halves)
    up_diagonal, down_diagonal = swap_core(up_far), swap_core(down_far)
    own_terms, near_terms, far_terms, diagonal_terms = gradients(
        tokens,
        labels,
        place,
        lax.axis_size("dp"),
        classifier,
        (up_short, up_near, up_far, up_diagonal),
        (down_short, down_near, down_far, down_diagonal),
    )
    from_diagonal = swap_core(diagonal_terms)
    from_near = swap_core(near_terms)
    away = (far_terms.astype(F32) + from_diagonal.astype(F32)).astype(BF16)
    shares = (from_near, swap_chip(away), own_terms)
    up_state, down_state = after((up_state, down_state), away)
    if members == DIRECT_MEMBERS:
        to_one, to_two = halves
        to_third, to_fourth = exchange_finish(up_state, down_state, halves, plan, members)
        up_candidates, down_candidates = (to_one, to_two, to_third), (to_third, to_two, to_fourth)
    else:
        up_candidates = (take_through_all(up_state, source, members),)
        down_candidates = (take_through_all(down_state, source, members),)

    new_state = adamw(
        choices,
        learn_rate,
        weight_decay,
        shares,
        (
            (up_param, up_first, up_second, up_short, *up_candidates),
            (down_param, down_first, down_second, down_short, *down_candidates),
        ),
    )
    return tuple(part[None] for part in new_state)


def solution(mesh):
    rows = P("member", "dp", None)
    placed = (
        P("member", "dp", None, None),
        P("member", "dp"),
        P(),
        P("member"),
        P("member"),
        P(),
        rows,
        rows,
        rows,
        rows,
        rows,
        rows,
    )
    return jax.shard_map(per_device, mesh=mesh, in_specs=placed, out_specs=(rows,) * 6, check_vma=False)
```

```python
import jax
import jax.numpy as jnp
from jax import lax
from jax.experimental import pallas as pl
from jax.experimental.pallas import tpu as pltpu
from jax.sharding import PartitionSpec as P

STEP = 1000
DIRECT_MEMBERS = 8
F32 = jnp.float32
BF16 = jnp.bfloat16


def after(value, token):
    return lax.optimization_barrier((value, token))[0]


def pairs_of(members):
    return [(one, two) for one in range(members) for two in range(one + 1, members)]


def plan_kernel(members, source_ref, me_ref, *refs):
    none = members * (members - 1) // 2
    places, takes, shared_out, flip, choices = refs[:4], refs[4:8], refs[8], refs[9], refs[10]

    def place_of(one, two):
        low, high = jnp.minimum(one, two), jnp.maximum(one, two)
        return jnp.right_shift(low * (2 * members - 1 - low), 1) + high - low - 1

    def flag(condition):
        return jnp.where(condition, 1, 0)

    zero = jnp.int32(0)
    taker_one = taker_two = source_one = source_two = zero
    for index in range(members):
        own = source_ref[index]
        taker_two = jnp.where(own != index, index, taker_two)
        source_two = jnp.where(own != index, own, source_two)
        back = members - 1 - index
        own = source_ref[back]
        taker_one = jnp.where(own != back, back, taker_one)
        source_one = jnp.where(own != back, own, source_one)
    me = me_ref[0]
    shared = source_one == source_two
    is_one, is_two = me == taker_one, me == taker_two
    first, second = place_of(source_one, taker_one), place_of(source_two, taker_two)
    places[0][0] = first
    places[1][0] = second
    places[2][0] = jnp.where(shared, place_of(taker_one, taker_two), first)
    places[3][0] = jnp.where(shared, none, second)
    takes[0][0] = flag(is_one)
    takes[1][0] = flag(is_two)
    takes[2][0] = flag(is_one | (shared & is_two))
    takes[3][0] = flag(is_two & jnp.logical_not(shared))
    shared_out[0] = flag(shared)
    flip[0] = flag(shared & is_two)
    choices[0] = jnp.where(is_one, 1, jnp.where(is_two, jnp.where(shared, 3, 2), 0))
    choices[1] = jnp.where(is_one, 1, jnp.where(is_two, jnp.where(shared, 2, 3), 0))


def find_plan(source, me):
    members = source.shape[0]
    in_smem = pl.BlockSpec(memory_space=pltpu.SMEM)
    found = pl.pallas_call(
        lambda *refs: plan_kernel(members, *refs),
        out_shape=[jax.ShapeDtypeStruct((size,), jnp.int32) for size in (1,) * 10 + (2,)],
        in_specs=[in_smem] * 2,
        out_specs=[in_smem] * 11,
    )(source, me.reshape(1))
    scalars = [scalar.reshape(()) for scalar in found[:9]]
    return scalars[:4], [take == 1 for take in scalars[4:8]], scalars[8] == 1, found[9], found[10]


def swap_pair(value, place, members):
    def branch(one, two):
        return lambda part: lax.ppermute(part, "member", [(one, two), (two, one)])

    return lax.switch(place, [branch(one, two) for one, two in pairs_of(members)] + [lambda part: part], value)


def exchange_round(index, value, other, plan, members):
    places, takes, shared = plan[:3]
    no = jnp.zeros((), jnp.bool_)
    now = (places[2 * index], takes[2 * index], shared if index else no)
    then = (places[2 * index + 1], takes[2 * index + 1], no if index else shared)

    def step(turn, carry):
        held, now, then = carry
        place, take, swap = now
        got = swap_pair(jnp.where(swap, other, value), place, members)
        return jnp.where(take, got, held), then, now

    return lax.fori_loop(0, 2, step, (value, now, then))[0]


def exchange_start(upper, lower, plan, members):
    places, _, shared = plan[:3]
    to_one = swap_pair(upper, places[0], members)
    to_two = swap_pair(after(jnp.where(shared, lower, upper), to_one), places[1], members)
    return to_one, to_two


def exchange_finish(lower, halves, plan, members):
    places, takes, shared = plan[:3]
    to_one, to_two = halves
    to_third = swap_pair(jnp.where(shared, jnp.where(takes[0], to_one, to_two), lower), places[2], members)
    to_fourth = swap_pair(after(lower, to_third), places[3], members)
    return to_third, to_fourth


def wide(value):
    half = value.shape[0] // 2
    return jnp.concatenate([value[:half], value[half:]], axis=1)


def take_through_all(value, source, members):
    flat = value.reshape(members, -1)
    parts = lax.all_to_all(flat, "member", split_axis=0, concat_axis=0, tiled=True)
    picked = jnp.take(parts, source, axis=0)
    return lax.all_to_all(picked, "member", split_axis=0, concat_axis=0, tiled=True).reshape(value.shape)


def swap_core(value):
    return lax.ppermute(value, "dp", [(0, 1), (1, 0), (2, 3), (3, 2)])


def swap_chip(value):
    return lax.ppermute(value, "dp", [(0, 2), (2, 0), (1, 3), (3, 1)])


TILE = 512
ROWS = 16


def gradient_kernel(
    images,
    patches,
    batch_total,
    place_ref,
    flip_ref,
    label_ref,
    tokens_hbm,
    classifier_hbm,
    first_own,
    first_near,
    first_far,
    first_diagonal,
    second_own,
    second_near,
    second_far,
    second_diagonal,
    own_out,
    near_out,
    far_out,
    diagonal_out,
    tokens_ref,
    classifier_ref,
    up_ref,
    down_ref,
    classes_ref,
    normed_ref,
    turned_ref,
    active_ref,
    slope_ref,
    residual_ref,
    inverse_ref,
    delta_ref,
    up_grad_ref,
    down_grad_ref,
    arrived,
    left,
):
    rows, features = residual_ref.shape
    hidden = up_ref.shape[1]
    share = first_own.shape[0]
    place = place_ref[0]
    up_scale = features ** (-0.5)
    down_scale = hidden ** (-0.5)

    tokens_copy = pltpu.make_async_copy(tokens_hbm, tokens_ref, arrived.at[12])
    classifier_copy = pltpu.make_async_copy(classifier_hbm, classifier_ref, arrived.at[13])
    tokens_copy.start()
    residual_ref[pl.ds(images * patches, rows - images * patches), :] = jnp.zeros(
        (rows - images * patches, features), F32
    )

    def fetch(up_blocks, down_blocks):
        up_copies, down_copies = [], []
        for step, block in enumerate(up_blocks):
            at = pl.multiple_of((place ^ step) * share, share)
            up_copies.append(pltpu.make_async_copy(block, up_ref.at[pl.ds(at, share), :], arrived.at[step]))
        for step, block in enumerate(down_blocks):
            for half in range(2):
                at = pl.multiple_of((place ^ step) * (2 * share) + half * share, share)
                down_copies.append(
                    pltpu.make_async_copy(
                        block.at[:, pl.ds(half * features, features)],
                        down_ref.at[pl.ds(at, share), :],
                        arrived.at[4 + 2 * step + half],
                    )
                )
        return up_copies, down_copies

    first_blocks = (first_own, first_near, first_far, first_diagonal)
    second_blocks = (second_own, second_near, second_far, second_diagonal)
    up_copies, down_copies = fetch(first_blocks, second_blocks)

    @pl.when(flip_ref[0] == 0)
    def _():
        for copy in up_copies + down_copies:
            copy.start()

    @pl.when(flip_ref[0] != 0)
    def _():
        for copies in fetch(second_blocks, first_blocks):
            for copy in copies:
                copy.start()

    classifier_copy.start()
    tokens_copy.wait()
    for step in range(patches):
        residual_ref[pl.ds(step * images, images), :] = tokens_ref[step].astype(F32)

    def norm_rows(step, carry):
        here = pl.ds(pl.multiple_of(step * ROWS, ROWS), ROWS)
        value = residual_ref[here, :]
        center = value - jnp.mean(value, axis=1, keepdims=True)
        spread = jnp.mean(center * center, axis=1, keepdims=True)
        normed_ref[here, :] = (center * lax.rsqrt(spread + 1e-06)).astype(BF16)
        return carry

    lax.fori_loop(0, rows // ROWS, norm_rows, 0, unroll=True)
    turned_ref[...] = normed_ref[...].T
    for copy in up_copies:
        copy.wait()

    def up_tile(step, carry):
        here = pl.ds(pl.multiple_of(step * TILE, TILE), TILE)
        preact = jnp.dot(normed_ref[...], up_ref[:, here], preferred_element_type=F32) * up_scale
        half = 0.5 * (1.0 + lax.erf(preact * 0.7071067811865476))
        active_ref[:, here] = (preact * half).astype(BF16)
        slope_ref[:, here] = half + preact * jnp.exp(-0.5 * preact * preact) * 0.3989422804014327
        return carry

    lax.fori_loop(0, hidden // TILE, up_tile, 0, unroll=3)
    for copy in down_copies:
        copy.wait()

    product = jnp.dot(active_ref[...], down_ref[...], preferred_element_type=F32)
    residual_ref[...] += product * down_scale

    def norm_out(step, total):
        here = pl.ds(pl.multiple_of(step * ROWS, ROWS), ROWS)
        value = residual_ref[here, :]
        center = value - jnp.mean(value, axis=1, keepdims=True)
        spread = jnp.mean(center * center, axis=1, keepdims=True)
        inverse = lax.rsqrt(spread + 1e-06)
        out = center * inverse
        residual_ref[here, :] = out
        inverse_ref[here, :] = jnp.broadcast_to(inverse, (ROWS, inverse_ref.shape[1]))
        return total + out[:8] + out[8:]

    total = lax.fori_loop(0, rows // ROWS, norm_out, jnp.zeros((8, features), F32), unroll=True)
    fold = images
    while fold < 8:
        total = total + jnp.concatenate([total[fold:], total[:fold]], axis=0)
        fold *= 2
    pooled = (total * (1.0 / patches)).astype(BF16)
    classifier_copy.wait()
    classes = classifier_ref.shape[0]
    classes_ref[...] = jnp.zeros_like(classes_ref)
    classes_ref[:classes, :] = classifier_ref[...].astype(F32)
    heads = classes_ref[...].astype(BF16)
    logits = lax.dot_general(pooled, heads, (((1,), (1,)), ((), ())), preferred_element_type=F32)
    kind = lax.broadcasted_iota(jnp.int32, logits.shape, 1)
    image_row = lax.broadcasted_iota(jnp.int32, logits.shape, 0)
    powered = jnp.where(kind < classes, jnp.exp(logits), 0.0)
    softmax_out = powered / jnp.sum(powered, axis=1, keepdims=True)
    label = jnp.full(logits.shape, -1, jnp.int32)
    for image in range(images):
        label = jnp.where(image_row % images == image, label_ref[image], label)
    onehot = jnp.where(kind == label, 1.0, 0.0)
    logit_delta = ((softmax_out - onehot) * (1.0 / batch_total)).astype(BF16)
    pool_delta = jnp.dot(logit_delta, heads, preferred_element_type=F32) * (1.0 / patches)
    pool_center = pool_delta - jnp.mean(pool_delta, axis=1, keepdims=True)

    token_delta = jnp.concatenate([pool_delta, pool_delta], axis=0)
    token_center = jnp.concatenate([pool_center, pool_center], axis=0)

    def delta_rows(step, carry):
        here = pl.ds(pl.multiple_of(step * ROWS, ROWS), ROWS)
        out = residual_ref[here, :]
        along = jnp.mean(token_delta * out, axis=1, keepdims=True)
        inverse = inverse_ref[here, :][:, :1]
        delta_ref[here, :] = (inverse * (token_center - out * along)).astype(BF16)
        return carry

    lax.fori_loop(0, rows // ROWS, delta_rows, 0, unroll=True)

    def back_tile(step, carry):
        here = pl.ds(pl.multiple_of(step * TILE, TILE), TILE)
        down_grad_ref[here, :] = (
            lax.dot_general(
                active_ref[:, here], delta_ref[...], (((0,), (0,)), ((), ())), preferred_element_type=F32
            )
            * down_scale
        ).astype(BF16)
        hidden_delta = lax.dot_general(
            delta_ref[...], down_ref[here, :], (((1,), (1,)), ((), ())), preferred_element_type=F32
        )
        preact_delta = (hidden_delta * down_scale * slope_ref[:, here]).astype(BF16)
        active_ref[:, here] = preact_delta
        return carry

    lax.fori_loop(0, hidden // TILE, back_tile, 0, unroll=3)

    outputs = (own_out, near_out, far_out, diagonal_out)
    leaving = []
    for step, block in enumerate(outputs):
        for half in range(2):
            at = pl.multiple_of((place ^ step) * (2 * share) + half * share, share)
            leaving.append(
                pltpu.make_async_copy(
                    down_grad_ref.at[pl.ds(at, share), :],
                    block.at[1, :, pl.ds(half * features, features)],
                    left.at[len(leaving)],
                )
            )
            leaving[-1].start()
    for tile in range(hidden // TILE):
        here = pl.ds(tile * TILE, TILE)
        up_grad_ref[:, here] = (
            jnp.dot(turned_ref[...], active_ref[:, here], preferred_element_type=F32) * up_scale
        ).astype(BF16)
        for step, block in enumerate(outputs):
            at = pl.multiple_of((place ^ step) * share, share)
            leaving.append(
                pltpu.make_async_copy(
                    up_grad_ref.at[pl.ds(at, share), here], block.at[0, :, here], left.at[len(leaving)]
                )
            )
            leaving[-1].start()
    for copy in leaving:
        copy.wait()


def gradients(tokens, labels, place, shards, flip, classifier, first_blocks, second_blocks):
    images, patches, features = tokens.shape
    share, hidden = first_blocks[0].shape
    rows = -(-images * patches // 64) * 64
    tokens = tokens.transpose(1, 0, 2)
    classifier = classifier.T
    in_smem = pl.BlockSpec(memory_space=pltpu.SMEM)
    anywhere = pl.BlockSpec(memory_space=pltpu.HBM)
    width = -(-classifier.shape[0] // 128) * 128
    return pl.pallas_call(
        lambda *refs: gradient_kernel(images, patches, images * shards, *refs),
        out_shape=[jax.ShapeDtypeStruct((2, share, hidden), BF16)] * 4,
        in_specs=[in_smem] * 3 + [anywhere] * 10,
        out_specs=[anywhere] * 4,
        scratch_shapes=[
            pltpu.VMEM(tokens.shape, BF16),
            pltpu.VMEM(classifier.shape, BF16),
            pltpu.VMEM((features, hidden), BF16),
            pltpu.VMEM((hidden, features), BF16),
            pltpu.VMEM((width, features), F32),
            pltpu.VMEM((rows, features), BF16),
            pltpu.VMEM((features, rows), BF16),
            pltpu.VMEM((rows, hidden), BF16),
            pltpu.VMEM((rows, hidden), F32),
            pltpu.VMEM((rows, features), F32),
            pltpu.VMEM((rows, 128), F32),
            pltpu.VMEM((rows, features), BF16),
            pltpu.VMEM((features, hidden), BF16),
            pltpu.VMEM((hidden, features), BF16),
            pltpu.SemaphoreType.DMA((14,)),
            pltpu.SemaphoreType.DMA((8 + 4 * (hidden // TILE),)),
        ],
        compiler_params=pltpu.CompilerParams(vmem_limit_bytes=56 * 1024 * 1024),
        cost_estimate=pl.CostEstimate(
            flops=10 * rows * features * hidden, bytes_accessed=12 * 1024 * 1024, transcendentals=0
        ),
    )(place.reshape(1), flip, labels, tokens, classifier, *first_blocks, *second_blocks)


CHUNKS = 4


def adamw_kernel(candidates, choice_ref, flip_ref, rate_ref, decay_ref, *refs):
    near, away, own = refs[:3]
    sides = (refs[3:6], refs[6:9])
    shorts = refs[9:11]
    at = 11 + 2 * candidates
    states = (refs[11 : 11 + candidates], refs[11 + candidates : at])
    outputs = refs[at : at + 6]
    buffers = refs[at + 6 : -2]
    arrived, left = refs[-2:]

    def spots(kind, chunk):
        rows, columns = sides[kind][0].shape
        step = rows // CHUNKS
        here = (pl.ds(chunk * step, step), slice(None))
        if not kind:
            return here, here
        half, part = divmod(chunk, CHUNKS // 2)
        return here, (pl.ds(part * step, step), pl.ds(half * columns, columns))

    def copies(kind, chunk):
        param, first, second = sides[kind]
        here, there = spots(kind, chunk)
        held = buffers[9 * kind : 9 * kind + 9]
        old, old_short, moment, variance, variance_short, terms_own, terms_near, terms_away = (
            buffer.at[here] for buffer in held[:8]
        )
        base = (kind * CHUNKS + chunk) * 6

        def copy(source, target, index):
            return pltpu.make_async_copy(source, target, arrived.at[base + index])

        fixed = [
            copy(own.at[(kind,) + there], terms_own, 3),
            copy(near.at[(kind,) + there], terms_near, 4),
            copy(away.at[(kind,) + there], terms_away, 5),
        ]
        kept = [copy(param.at[here], old, 0), copy(first.at[here], moment, 1), copy(second.at[here], variance, 2)]

        def moved(index):
            return [
                copy(states[kind][index].at[(0,) + there], moment, 1),
                copy(states[kind][index].at[(1,) + there], variance_short, 2),
            ]

        def taken(flipped):
            return copy(shorts[kind ^ flipped].at[there], old_short, 0)

        return fixed, kept, moved, taken

    choices = [choice_ref[0], choice_ref[1]]
    work = [(kind, chunk) for kind in range(2) for chunk in range(CHUNKS)]
    for kind, chunk in work:
        fixed, kept, moved, taken = copies(kind, chunk)

        @pl.when(choices[kind] == 0)
        def _():
            for copy in kept:
                copy.start()

        for index in range(candidates):

            @pl.when(choices[kind] == index + 1)
            def _():
                for copy in moved(index):
                    copy.start()

        for flipped in range(2):

            @pl.when((choices[kind] != 0) & (flip_ref[0] == flipped))
            def _():
                taken(flipped).start()

        for copy in fixed:
            copy.start()

    rate, decay = rate_ref[0], decay_ref[0]
    leaving = []
    for kind, chunk in work:
        fixed, kept, moved, taken = copies(kind, chunk)

        @pl.when(choices[kind] == 0)
        def _():
            for copy in kept:
                copy.wait()

        @pl.when(choices[kind] != 0)
        def _():
            for copy in moved(0):
                copy.wait()
            taken(0).wait()

        for copy in fixed:
            copy.wait()
        here, _ = spots(kind, chunk)
        held = buffers[9 * kind : 9 * kind + 9]
        old, old_short, moment_in, variance_in, variance_short, terms_own, terms_near, terms_away, moment_out = held
        own_state = choices[kind] == 0
        before = jnp.where(own_state, old[here], old_short[here].astype(F32))
        variance = jnp.where(own_state, variance_in[here], variance_short[here].astype(F32))
        gradient = terms_own[here].astype(F32) + terms_near[here].astype(F32) + terms_away[here].astype(F32)
        moment = 0.9 * moment_in[here].astype(F32) + 0.1 * gradient
        variance = 0.999 * variance + 0.001 * gradient * gradient
        root = jnp.sqrt(variance * (1.0 / (1.0 - 0.999**STEP))) + 1e-08
        update = moment * (1.0 / (1.0 - 0.9**STEP)) / root + decay * before
        old[here] = before - rate * update
        moment_out[here] = moment.astype(BF16)
        variance_in[here] = variance
        for source, target in zip((old, moment_out, variance_in), outputs[3 * kind : 3 * kind + 3]):
            leaving.append(pltpu.make_async_copy(source.at[here], target.at[here], left.at[len(leaving)]))
            leaving[-1].start()
    for copy in leaving:
        copy.wait()


def adamw(choices, rate, decay, shares, sides, shorts, flip, states):
    candidates = len(states[0])
    in_smem = pl.BlockSpec(memory_space=pltpu.SMEM)
    anywhere = pl.BlockSpec(memory_space=pltpu.HBM)
    outputs, buffers = [], []
    for side in sides:
        shape = side[0].shape
        outputs += [jax.ShapeDtypeStruct(shape, kind) for kind in (F32, BF16, F32)]
        buffers += [pltpu.VMEM(shape, kind) for kind in (F32, BF16, BF16, F32) + (BF16,) * 5]
    count = 2 * CHUNKS
    return pl.pallas_call(
        lambda *refs: adamw_kernel(candidates, *refs),
        out_shape=outputs,
        in_specs=[in_smem] * 4 + [anywhere] * (11 + 2 * candidates),
        out_specs=[anywhere] * 6,
        scratch_shapes=buffers + [pltpu.SemaphoreType.DMA((6 * count,)), pltpu.SemaphoreType.DMA((3 * count,))],
        compiler_params=pltpu.CompilerParams(vmem_limit_bytes=56 * 1024 * 1024),
        cost_estimate=pl.CostEstimate(
            flops=40 * sides[0][0].size, bytes_accessed=16 * 1024 * 1024, transcendentals=0
        ),
    )(choices, flip, rate, decay, *shares, *sides[0], *sides[1], *shorts, *states[0], *states[1])


def per_device(
    tokens,
    labels,
    source,
    learn_rate,
    weight_decay,
    classifier,
    up_param,
    up_first,
    up_second,
    down_param,
    down_first,
    down_second,
):
    members = lax.axis_size("member")
    me = lax.axis_index("member")
    place = lax.axis_index("dp")
    tokens, labels = tokens[0], labels[0]
    up_param, up_first, up_second = up_param[0], up_first[0], up_second[0]
    down_param, down_first, down_second = down_param[0], down_first[0], down_second[0]
    up_own, down_own = up_param.astype(BF16), wide(down_param.astype(BF16))
    up_state = jnp.stack([up_first, up_second.astype(BF16)])
    down_state = jnp.stack([wide(down_first), wide(down_second.astype(BF16))])
    direct = members == DIRECT_MEMBERS
    if direct:
        plan = find_plan(source, me)
        flip, choices = plan[3:]
        first = exchange_round(0, up_own, down_own, plan, members)
    else:
        flip = jnp.zeros((1,), jnp.int32)
        choices = jnp.where(source[me] != me, jnp.ones((2,), jnp.int32), 0)
        first = take_through_all(up_own, source, members)
    first_far, first_near = swap_chip(first), swap_core(first)
    if direct:
        second = exchange_round(1, down_own, first, plan, members)
    else:
        second = take_through_all(down_own, source, members)
    second_far, second_near = swap_chip(second), swap_core(second)
    up_state, down_state = after((up_state, down_state), (first, second))
    if direct:
        halves = exchange_start(up_state, down_state, plan, members)
        first_far, second_far = after((first_far, second_far), halves)
    else:
        halves = (take_through_all(up_state, source, members),)
    own_terms, near_terms, far_terms, diagonal_terms = gradients(
        tokens,
        labels,
        place,
        lax.axis_size("dp"),
        flip,
        classifier,
        (first, first_near, first_far, swap_core(first_far)),
        (second, second_near, second_far, swap_core(second_far)),
    )
    from_diagonal = swap_core(diagonal_terms)
    from_near = swap_core(near_terms)
    away = (far_terms.astype(F32) + from_diagonal.astype(F32)).astype(BF16)
    shares = (from_near, swap_chip(away), own_terms)
    halves, down_state = after((halves, down_state), away)
    if direct:
        to_one, to_two = halves
        to_third, to_fourth = exchange_finish(down_state, halves, plan, members)
        states = ((to_one, to_two, to_third), (to_third, to_two, to_fourth))
    else:
        states = (halves, (take_through_all(down_state, source, members),))
    new_state = adamw(
        choices,
        learn_rate,
        weight_decay,
        shares,
        ((up_param, up_first, up_second), (down_param, down_first, down_second)),
        (first, second),
        flip,
        states,
    )
    return tuple(part[None] for part in new_state)


def solution(mesh):
    rows = P("member", "dp", None)
    placed = (
        P("member", "dp", None, None),
        P("member", "dp"),
        P(),
        P("member"),
        P("member"),
        P(),
        rows,
        rows,
        rows,
        rows,
        rows,
        rows,
    )
    return jax.shard_map(per_device, mesh=mesh, in_specs=placed, out_specs=(rows,) * 6, check_vma=False)
```

```python
import jax
import jax.numpy as jnp
from jax import lax
from jax.experimental import pallas as pl
from jax.experimental.pallas import tpu as pltpu
from jax.sharding import PartitionSpec as P

STEP = 1000
DIRECT_MEMBERS = 8
F32 = jnp.float32
BF16 = jnp.bfloat16


def after(value, token):
    return lax.optimization_barrier((value, token))[0]


def pairs_of(members):
    return [(one, two) for one in range(members) for two in range(one + 1, members)]


def plan_kernel(members, source_ref, me_ref, first, second, third, fourth, shared, is_one, loses, choices):
    none = members * (members - 1) // 2

    def place_of(one, two):
        low, high = jnp.minimum(one, two), jnp.maximum(one, two)
        return jnp.right_shift(low * (2 * members - 1 - low), 1) + high - low - 1

    zero = jnp.int32(0)
    taker_one = taker_two = source_one = source_two = zero
    for index in range(members):
        own = source_ref[index]
        takes = own != index
        taker_two = jnp.where(takes, index, taker_two)
        source_two = jnp.where(takes, own, source_two)
        back = members - 1 - index
        own = source_ref[back]
        takes = own != back
        taker_one = jnp.where(takes, back, taker_one)
        source_one = jnp.where(takes, own, source_one)
    same = source_one == source_two
    first[0] = place_of(source_one, taker_one)
    second[0] = place_of(source_two, taker_two)
    third[0] = jnp.where(same, place_of(taker_one, taker_two), place_of(source_one, taker_one))
    fourth[0] = jnp.where(same, none, place_of(source_two, taker_two))
    shared[0] = jnp.where(same, 1, 0)
    me = me_ref[0]
    is_one[0] = jnp.where(me == taker_one, 1, 0)
    loses[0] = jnp.where((me == taker_one) | (me == taker_two), 1, 0)
    two_or = jnp.where(me == taker_two, jnp.where(same, 3, 2), 0)
    choices[0] = jnp.where(me == taker_one, 1, two_or)
    two_or = jnp.where(me == taker_two, jnp.where(same, 2, 3), 0)
    choices[1] = jnp.where(me == taker_one, 1, two_or)


def find_plan(source, me):
    members = source.shape[0]
    scalars = pl.pallas_call(
        lambda *refs: plan_kernel(members, *refs),
        out_shape=[jax.ShapeDtypeStruct((1,), jnp.int32)] * 7 + [jax.ShapeDtypeStruct((2,), jnp.int32)],
        in_specs=[pl.BlockSpec(memory_space=pltpu.SMEM)] * 2,
        out_specs=[pl.BlockSpec(memory_space=pltpu.SMEM)] * 8,
    )(source, me.reshape(1))
    first, second, third, fourth, shared, is_one, loses = (scalar.reshape(()) for scalar in scalars[:7])
    return first, second, third, fourth, shared == 1, is_one == 1, loses == 1, scalars[7]


def swap_pair(value, place, members):
    def branch(one, two):
        return lambda parts: jax.tree.map(lambda part: lax.ppermute(part, "member", [(one, two), (two, one)]), parts)

    return lax.switch(place, [branch(one, two) for one, two in pairs_of(members)] + [lambda parts: parts], value)


def exchange_start(upper, lower, plan, members):
    first, second, _, _, shared = plan[:5]
    to_one = swap_pair(upper, first, members)
    to_two = swap_pair(after(jnp.where(shared, lower, upper), to_one), second, members)
    return to_one, to_two


def exchange_finish(upper, lower, halves, plan, members):
    to_one, to_two = halves
    third, fourth, shared, is_one = plan[2:6]
    to_third = swap_pair(jnp.where(shared, jnp.where(is_one, to_one, to_two), lower), third, members)
    to_fourth = swap_pair(after(lower, to_third), fourth, members)
    return to_third, to_fourth


def exchange_weights(up, down, plan, members):
    first, second, third, _, shared, is_one, loses = plan[:7]

    def whole(up, down):
        own = jnp.stack([up.astype(BF16), wide(down.astype(BF16))])
        to_one = swap_pair(own, first, members)
        to_two = swap_pair(after(own, to_one), second, members)
        now = jnp.where(loses, jnp.where(is_one, to_one, to_two), own)
        return now[0], now[1]

    def halves(up, down):
        upper, lower = up.astype(BF16), wide(down.astype(BF16))

        to_one = swap_pair(upper, first, members)
        to_two = swap_pair(after(lower, to_one), second, members)
        mine = jnp.where(is_one, to_one, to_two)
        got = swap_pair(mine, third, members)
        return (
            jnp.where(loses, jnp.where(is_one, mine, got), upper),
            jnp.where(loses, jnp.where(is_one, got, mine), lower),
        )

    return lax.cond(shared, halves, whole, up, down)


def wide(value):
    half = value.shape[0] // 2
    return jnp.concatenate([value[:half], value[half:]], axis=1)


def take_through_all(value, source, members):
    flat = value.reshape(members, -1)
    parts = lax.all_to_all(flat, "member", split_axis=0, concat_axis=0, tiled=True)
    picked = jnp.take(parts, source, axis=0)
    return lax.all_to_all(picked, "member", split_axis=0, concat_axis=0, tiled=True).reshape(value.shape)


def swap_core(value):
    return lax.ppermute(value, "dp", [(0, 1), (1, 0), (2, 3), (3, 2)])


def swap_chip(value):
    return lax.ppermute(value, "dp", [(0, 2), (2, 0), (1, 3), (3, 1)])


TILE = 512
ROWS = 16


def gradient_kernel(
    images,
    patches,
    batch_total,
    place_ref,
    label_ref,
    tokens_hbm,
    classifier_hbm,
    up_own,
    up_near,
    up_far,
    up_diagonal,
    down_own,
    down_near,
    down_far,
    down_diagonal,
    own_out,
    near_out,
    far_out,
    diagonal_out,
    tokens_ref,
    classifier_ref,
    up_ref,
    down_ref,
    classes_ref,
    normed_ref,
    turned_ref,
    active_ref,
    slope_ref,
    residual_ref,
    inverse_ref,
    delta_ref,
    up_grad_ref,
    down_grad_ref,
    arrived,
    left,
):
    rows, features = residual_ref.shape
    hidden = up_ref.shape[1]
    share = up_own.shape[0]
    place = place_ref[0]
    up_scale = features ** (-0.5)
    down_scale = hidden ** (-0.5)

    tokens_copy = pltpu.make_async_copy(tokens_hbm, tokens_ref, arrived.at[12])
    classifier_copy = pltpu.make_async_copy(classifier_hbm, classifier_ref, arrived.at[13])
    tokens_copy.start()
    residual_ref[pl.ds(images * patches, rows - images * patches), :] = jnp.zeros(
        (rows - images * patches, features), F32
    )
    up_copies, down_copies = [], []
    for step, block in enumerate((up_own, up_near, up_far, up_diagonal)):
        at = pl.multiple_of((place ^ step) * share, share)
        up_copies.append(pltpu.make_async_copy(block, up_ref.at[pl.ds(at, share), :], arrived.at[step]))
    for step, block in enumerate((down_own, down_near, down_far, down_diagonal)):
        for half in range(2):
            at = pl.multiple_of((place ^ step) * (2 * share) + half * share, share)
            down_copies.append(
                pltpu.make_async_copy(
                    block.at[:, pl.ds(half * features, features)],
                    down_ref.at[pl.ds(at, share), :],
                    arrived.at[4 + 2 * step + half],
                )
            )
    for copy in up_copies + down_copies + [classifier_copy]:
        copy.start()

    tokens_copy.wait()
    for step in range(patches):
        residual_ref[pl.ds(step * images, images), :] = tokens_ref[step].astype(F32)

    def norm_rows(step, carry):
        here = pl.ds(pl.multiple_of(step * ROWS, ROWS), ROWS)
        value = residual_ref[here, :]
        center = value - jnp.mean(value, axis=1, keepdims=True)
        spread = jnp.mean(center * center, axis=1, keepdims=True)
        normed_ref[here, :] = (center * lax.rsqrt(spread + 1e-06)).astype(BF16)
        return carry

    lax.fori_loop(0, rows // ROWS, norm_rows, 0, unroll=True)
    turned_ref[...] = normed_ref[...].T
    for copy in up_copies:
        copy.wait()

    def up_tile(step, carry):
        here = pl.ds(pl.multiple_of(step * TILE, TILE), TILE)
        preact = jnp.dot(normed_ref[...], up_ref[:, here], preferred_element_type=F32) * up_scale
        half = 0.5 * (1.0 + lax.erf(preact * 0.7071067811865476))
        active_ref[:, here] = (preact * half).astype(BF16)
        slope_ref[:, here] = half + preact * jnp.exp(-0.5 * preact * preact) * 0.3989422804014327
        return carry

    lax.fori_loop(0, hidden // TILE, up_tile, 0, unroll=3)
    for copy in down_copies:
        copy.wait()

    product = jnp.dot(active_ref[...], down_ref[...], preferred_element_type=F32)
    residual_ref[...] += product * down_scale

    def norm_out(step, total):
        here = pl.ds(pl.multiple_of(step * ROWS, ROWS), ROWS)
        value = residual_ref[here, :]
        center = value - jnp.mean(value, axis=1, keepdims=True)
        spread = jnp.mean(center * center, axis=1, keepdims=True)
        inverse = lax.rsqrt(spread + 1e-06)
        out = center * inverse
        residual_ref[here, :] = out
        inverse_ref[here, :] = jnp.broadcast_to(inverse, (ROWS, inverse_ref.shape[1]))
        return total + out[:8] + out[8:]

    total = lax.fori_loop(0, rows // ROWS, norm_out, jnp.zeros((8, features), F32), unroll=True)
    fold = images
    while fold < 8:
        total = total + jnp.concatenate([total[fold:], total[:fold]], axis=0)
        fold *= 2
    pooled = (total * (1.0 / patches)).astype(BF16)
    classifier_copy.wait()
    classes = classifier_ref.shape[0]
    classes_ref[...] = jnp.zeros_like(classes_ref)
    classes_ref[:classes, :] = classifier_ref[...].astype(F32)
    heads = classes_ref[...].astype(BF16)
    logits = lax.dot_general(pooled, heads, (((1,), (1,)), ((), ())), preferred_element_type=F32)
    kind = lax.broadcasted_iota(jnp.int32, logits.shape, 1)
    image_row = lax.broadcasted_iota(jnp.int32, logits.shape, 0)
    powered = jnp.where(kind < classes, jnp.exp(logits), 0.0)
    softmax_out = powered / jnp.sum(powered, axis=1, keepdims=True)
    label = jnp.full(logits.shape, -1, jnp.int32)
    for image in range(images):
        label = jnp.where(image_row % images == image, label_ref[image], label)
    onehot = jnp.where(kind == label, 1.0, 0.0)
    logit_delta = ((softmax_out - onehot) * (1.0 / batch_total)).astype(BF16)
    pool_delta = jnp.dot(logit_delta, heads, preferred_element_type=F32) * (1.0 / patches)
    pool_center = pool_delta - jnp.mean(pool_delta, axis=1, keepdims=True)

    token_delta = jnp.concatenate([pool_delta, pool_delta], axis=0)
    token_center = jnp.concatenate([pool_center, pool_center], axis=0)

    def delta_rows(step, carry):
        here = pl.ds(pl.multiple_of(step * ROWS, ROWS), ROWS)
        out = residual_ref[here, :]
        along = jnp.mean(token_delta * out, axis=1, keepdims=True)
        inverse = inverse_ref[here, :][:, :1]
        delta_ref[here, :] = (inverse * (token_center - out * along)).astype(BF16)
        return carry

    lax.fori_loop(0, rows // ROWS, delta_rows, 0, unroll=True)

    def back_tile(step, carry):
        here = pl.ds(pl.multiple_of(step * TILE, TILE), TILE)
        down_grad_ref[here, :] = (
            lax.dot_general(
                active_ref[:, here], delta_ref[...], (((0,), (0,)), ((), ())), preferred_element_type=F32
            )
            * down_scale
        ).astype(BF16)
        hidden_delta = lax.dot_general(
            delta_ref[...], down_ref[here, :], (((1,), (1,)), ((), ())), preferred_element_type=F32
        )
        preact_delta = (hidden_delta * down_scale * slope_ref[:, here]).astype(BF16)
        active_ref[:, here] = preact_delta
        return carry

    lax.fori_loop(0, hidden // TILE, back_tile, 0, unroll=3)

    outputs = (own_out, near_out, far_out, diagonal_out)
    leaving = []
    for step, block in enumerate(outputs):
        for half in range(2):
            at = pl.multiple_of((place ^ step) * (2 * share) + half * share, share)
            leaving.append(
                pltpu.make_async_copy(
                    down_grad_ref.at[pl.ds(at, share), :],
                    block.at[1, :, pl.ds(half * features, features)],
                    left.at[len(leaving)],
                )
            )
            leaving[-1].start()
    for tile in range(hidden // TILE):
        here = pl.ds(tile * TILE, TILE)
        up_grad_ref[:, here] = (
            jnp.dot(turned_ref[...], active_ref[:, here], preferred_element_type=F32) * up_scale
        ).astype(BF16)
        for step, block in enumerate(outputs):
            at = pl.multiple_of((place ^ step) * share, share)
            leaving.append(
                pltpu.make_async_copy(
                    up_grad_ref.at[pl.ds(at, share), here], block.at[0, :, here], left.at[len(leaving)]
                )
            )
            leaving[-1].start()
    for copy in leaving:
        copy.wait()


def gradients(tokens, labels, place, shards, classifier, up_blocks, down_blocks):
    images, patches, features = tokens.shape
    share, hidden = up_blocks[0].shape
    rows = -(-images * patches // 64) * 64
    tokens = tokens.transpose(1, 0, 2)
    classifier = classifier.T
    in_smem = pl.BlockSpec(memory_space=pltpu.SMEM)
    anywhere = pl.BlockSpec(memory_space=pltpu.HBM)
    width = -(-classifier.shape[0] // 128) * 128
    return pl.pallas_call(
        lambda *refs: gradient_kernel(images, patches, images * shards, *refs),
        out_shape=[jax.ShapeDtypeStruct((2, share, hidden), BF16)] * 4,
        in_specs=[in_smem] * 2 + [anywhere] * 10,
        out_specs=[anywhere] * 4,
        scratch_shapes=[
            pltpu.VMEM(tokens.shape, BF16),
            pltpu.VMEM(classifier.shape, BF16),
            pltpu.VMEM((features, hidden), BF16),
            pltpu.VMEM((hidden, features), BF16),
            pltpu.VMEM((width, features), F32),
            pltpu.VMEM((rows, features), BF16),
            pltpu.VMEM((features, rows), BF16),
            pltpu.VMEM((rows, hidden), BF16),
            pltpu.VMEM((rows, hidden), F32),
            pltpu.VMEM((rows, features), F32),
            pltpu.VMEM((rows, 128), F32),
            pltpu.VMEM((rows, features), BF16),
            pltpu.VMEM((features, hidden), BF16),
            pltpu.VMEM((hidden, features), BF16),
            pltpu.SemaphoreType.DMA((14,)),
            pltpu.SemaphoreType.DMA((8 + 4 * (hidden // TILE),)),
        ],
        compiler_params=pltpu.CompilerParams(vmem_limit_bytes=56 * 1024 * 1024),
        cost_estimate=pl.CostEstimate(
            flops=10 * rows * features * hidden, bytes_accessed=12 * 1024 * 1024, transcendentals=0
        ),
    )(place.reshape(1), labels, tokens, classifier, *up_blocks, *down_blocks)


CHUNKS = 4


def adamw_kernel(candidates, choice_ref, rate_ref, decay_ref, *refs):
    near, away, own = refs[:3]
    sides = []
    at = 3
    for _ in range(2):
        sides.append(refs[at : at + 4 + candidates])
        at += 4 + candidates
    outputs = refs[at : at + 6]
    buffers = refs[at + 6 : -2]
    arrived, left = refs[-2:]

    def spots(kind, chunk):
        rows, columns = sides[kind][0].shape
        step = rows // CHUNKS
        here = (pl.ds(chunk * step, step), slice(None))
        if not kind:
            return here, here
        half, part = divmod(chunk, CHUNKS // 2)
        return here, (pl.ds(part * step, step), pl.ds(half * columns, columns))

    def copies(kind, chunk):
        param, first, second, short = sides[kind][:4]
        taken = sides[kind][4:]
        here, there = spots(kind, chunk)
        held = buffers[9 * kind : 9 * kind + 9]
        old, old_short, moment, variance, variance_short, terms_own, terms_near, terms_away = (
            buffer.at[here] for buffer in held[:8]
        )
        base = (kind * CHUNKS + chunk) * 6

        def copy(source, target, index):
            return pltpu.make_async_copy(source, target, arrived.at[base + index])

        fixed = [
            copy(own.at[(kind,) + there], terms_own, 3),
            copy(near.at[(kind,) + there], terms_near, 4),
            copy(away.at[(kind,) + there], terms_away, 5),
        ]
        kept = [copy(param.at[here], old, 0), copy(first.at[here], moment, 1), copy(second.at[here], variance, 2)]

        def moved(index):
            return [
                copy(short.at[there], old_short, 0),
                copy(taken[index].at[(0,) + there], moment, 1),
                copy(taken[index].at[(1,) + there], variance_short, 2),
            ]

        return fixed, kept, moved

    choices = [choice_ref[0], choice_ref[1]]
    work = [(kind, chunk) for kind in range(2) for chunk in range(CHUNKS)]
    for kind, chunk in work:
        fixed, kept, moved = copies(kind, chunk)

        @pl.when(choices[kind] == 0)
        def _():
            for copy in kept:
                copy.start()

        for index in range(candidates):

            @pl.when(choices[kind] == index + 1)
            def _():
                for copy in moved(index):
                    copy.start()

        for copy in fixed:
            copy.start()

    rate, decay = rate_ref[0], decay_ref[0]
    leaving = []
    for kind, chunk in work:
        fixed, kept, moved = copies(kind, chunk)

        @pl.when(choices[kind] == 0)
        def _():
            for copy in kept:
                copy.wait()

        @pl.when(choices[kind] != 0)
        def _():
            for copy in moved(0):
                copy.wait()

        for copy in fixed:
            copy.wait()
        here, _ = spots(kind, chunk)
        held = buffers[9 * kind : 9 * kind + 9]
        old, old_short, moment_in, variance_in, variance_short, terms_own, terms_near, terms_away, moment_out = held
        own_state = choices[kind] == 0
        before = jnp.where(own_state, old[here], old_short[here].astype(F32))
        variance = jnp.where(own_state, variance_in[here], variance_short[here].astype(F32))
        gradient = terms_own[here].astype(F32) + terms_near[here].astype(F32) + terms_away[here].astype(F32)
        moment = 0.9 * moment_in[here].astype(F32) + 0.1 * gradient
        variance = 0.999 * variance + 0.001 * gradient * gradient
        root = jnp.sqrt(variance * (1.0 / (1.0 - 0.999**STEP))) + 1e-08
        update = moment * (1.0 / (1.0 - 0.9**STEP)) / root + decay * before
        old[here] = before - rate * update
        moment_out[here] = moment.astype(BF16)
        variance_in[here] = variance
        for source, target in zip((old, moment_out, variance_in), outputs[3 * kind : 3 * kind + 3]):
            leaving.append(pltpu.make_async_copy(source.at[here], target.at[here], left.at[len(leaving)]))
            leaving[-1].start()
    for copy in leaving:
        copy.wait()


def adamw(choices, rate, decay, shares, sides):
    candidates = len(sides[0]) - 4
    in_smem = pl.BlockSpec(memory_space=pltpu.SMEM)
    anywhere = pl.BlockSpec(memory_space=pltpu.HBM)
    outputs, buffers = [], []
    for side in sides:
        shape = side[0].shape
        outputs += [jax.ShapeDtypeStruct(shape, kind) for kind in (F32, BF16, F32)]
        buffers += [pltpu.VMEM(shape, kind) for kind in (F32, BF16, BF16, F32) + (BF16,) * 5]
    count = 2 * CHUNKS
    return pl.pallas_call(
        lambda *refs: adamw_kernel(candidates, *refs),
        out_shape=outputs,
        in_specs=[in_smem] * 3 + [anywhere] * (3 + 2 * (4 + candidates)),
        out_specs=[anywhere] * 6,
        scratch_shapes=buffers + [pltpu.SemaphoreType.DMA((6 * count,)), pltpu.SemaphoreType.DMA((3 * count,))],
        compiler_params=pltpu.CompilerParams(vmem_limit_bytes=56 * 1024 * 1024),
        cost_estimate=pl.CostEstimate(
            flops=40 * sides[0][0].size, bytes_accessed=16 * 1024 * 1024, transcendentals=0
        ),
    )(choices, rate, decay, *shares, *sides[0], *sides[1])


def per_device(
    tokens,
    labels,
    source,
    learn_rate,
    weight_decay,
    classifier,
    up_param,
    up_first,
    up_second,
    down_param,
    down_first,
    down_second,
):
    members = lax.axis_size("member")
    me = lax.axis_index("member")
    place = lax.axis_index("dp")
    tokens, labels = tokens[0], labels[0]
    up_param, up_first, up_second = up_param[0], up_first[0], up_second[0]
    down_param, down_first, down_second = down_param[0], down_first[0], down_second[0]
    up_state = jnp.stack([up_first, up_second.astype(BF16)])
    down_state = jnp.stack([wide(down_first), wide(down_second.astype(BF16))])
    if members == DIRECT_MEMBERS:
        plan = find_plan(source, me)
        choices = plan[7]
        up_short, down_short = exchange_weights(up_param, down_param, plan, members)
    else:
        up_short = take_through_all(up_param.astype(BF16), source, members)
        down_short = take_through_all(wide(down_param.astype(BF16)), source, members)
        choices = jnp.where(source[me] != me, jnp.ones((2,), jnp.int32), 0)

    up_far, down_far = swap_chip(up_short), swap_chip(down_short)
    up_near, down_near = swap_core(up_short), swap_core(down_short)
    up_state, down_state = after((up_state, down_state), (up_short, down_short))
    if members == DIRECT_MEMBERS:
        halves = exchange_start(up_state, down_state, plan, members)
        up_far, down_far = after((up_far, down_far), halves)
    up_diagonal, down_diagonal = swap_core(up_far), swap_core(down_far)
    own_terms, near_terms, far_terms, diagonal_terms = gradients(
        tokens,
        labels,
        place,
        lax.axis_size("dp"),
        classifier,
        (up_short, up_near, up_far, up_diagonal),
        (down_short, down_near, down_far, down_diagonal),
    )
    from_diagonal = swap_core(diagonal_terms)
    from_near = swap_core(near_terms)
    away = (far_terms.astype(F32) + from_diagonal.astype(F32)).astype(BF16)
    shares = (from_near, swap_chip(away), own_terms)
    up_state, down_state = after((up_state, down_state), away)
    if members == DIRECT_MEMBERS:
        to_one, to_two = halves
        to_third, to_fourth = exchange_finish(up_state, down_state, halves, plan, members)
        up_candidates, down_candidates = (to_one, to_two, to_third), (to_third, to_two, to_fourth)
    else:
        up_candidates = (take_through_all(up_state, source, members),)
        down_candidates = (take_through_all(down_state, source, members),)

    new_state = adamw(
        choices,
        learn_rate,
        weight_decay,
        shares,
        (
            (up_param, up_first, up_second, up_short, *up_candidates),
            (down_param, down_first, down_second, down_short, *down_candidates),
        ),
    )
    return tuple(part[None] for part in new_state)


def solution(mesh):
    rows = P("member", "dp", None)
    placed = (
        P("member", "dp", None, None),
        P("member", "dp"),
        P(),
        P("member"),
        P("member"),
        P(),
        rows,
        rows,
        rows,
        rows,
        rows,
        rows,
    )
    return jax.shard_map(per_device, mesh=mesh, in_specs=placed, out_specs=(rows,) * 6, check_vma=False)
```

```python
import jax
import jax.numpy as jnp
from jax import lax
from jax.experimental import pallas as pl
from jax.experimental.pallas import tpu as pltpu
from jax.sharding import PartitionSpec as P

STEP = 1000
DIRECT_MEMBERS = 8
F32 = jnp.float32
BF16 = jnp.bfloat16


def after(value, token):
    return lax.optimization_barrier((value, token))[0]


def pairs_of(members):
    return [(one, two) for one in range(members) for two in range(one + 1, members)]


def plan_kernel(members, source_ref, me_ref, first, second, third, fourth, shared, is_one, loses, choices):
    none = members * (members - 1) // 2

    def place_of(one, two):
        low, high = jnp.minimum(one, two), jnp.maximum(one, two)
        return jnp.right_shift(low * (2 * members - 1 - low), 1) + high - low - 1

    zero = jnp.int32(0)
    taker_one = taker_two = source_one = source_two = zero
    for index in range(members):
        own = source_ref[index]
        takes = own != index
        taker_two = jnp.where(takes, index, taker_two)
        source_two = jnp.where(takes, own, source_two)
        back = members - 1 - index
        own = source_ref[back]
        takes = own != back
        taker_one = jnp.where(takes, back, taker_one)
        source_one = jnp.where(takes, own, source_one)
    same = source_one == source_two
    first[0] = place_of(source_one, taker_one)
    second[0] = place_of(source_two, taker_two)
    third[0] = jnp.where(same, place_of(taker_one, taker_two), place_of(source_one, taker_one))
    fourth[0] = jnp.where(same, none, place_of(source_two, taker_two))
    shared[0] = jnp.where(same, 1, 0)
    me = me_ref[0]
    is_one[0] = jnp.where(me == taker_one, 1, 0)
    loses[0] = jnp.where((me == taker_one) | (me == taker_two), 1, 0)
    two_or = jnp.where(me == taker_two, jnp.where(same, 3, 2), 0)
    choices[0] = jnp.where(me == taker_one, 1, two_or)
    two_or = jnp.where(me == taker_two, jnp.where(same, 2, 3), 0)
    choices[1] = jnp.where(me == taker_one, 1, two_or)


def find_plan(source, me):
    members = source.shape[0]
    scalars = pl.pallas_call(
        lambda *refs: plan_kernel(members, *refs),
        out_shape=[jax.ShapeDtypeStruct((1,), jnp.int32)] * 7 + [jax.ShapeDtypeStruct((2,), jnp.int32)],
        in_specs=[pl.BlockSpec(memory_space=pltpu.SMEM)] * 2,
        out_specs=[pl.BlockSpec(memory_space=pltpu.SMEM)] * 8,
    )(source, me.reshape(1))
    first, second, third, fourth, shared, is_one, loses = (scalar.reshape(()) for scalar in scalars[:7])
    return first, second, third, fourth, shared == 1, is_one == 1, loses == 1, scalars[7]


def swap_pair(value, place, members):
    def branch(one, two):
        return lambda parts: jax.tree.map(lambda part: lax.ppermute(part, "member", [(one, two), (two, one)]), parts)

    return lax.switch(place, [branch(one, two) for one, two in pairs_of(members)] + [lambda parts: parts], value)


def exchange_start(upper, lower, plan, members):
    first, second, _, _, shared = plan[:5]
    to_one = swap_pair(upper, first, members)
    to_two = swap_pair(after(jnp.where(shared, lower, upper), to_one), second, members)
    return to_one, to_two


def exchange_finish(upper, lower, halves, plan, members):
    to_one, to_two = halves
    third, fourth, shared, is_one = plan[2:6]
    to_third = swap_pair(jnp.where(shared, jnp.where(is_one, to_one, to_two), lower), third, members)
    to_fourth = swap_pair(after(lower, to_third), fourth, members)
    return to_third, to_fourth


def exchange_weights(up, down, plan, members):
    first, second, third, _, shared, is_one, loses = plan[:7]

    def whole(up, down):
        own = jnp.stack([up.astype(BF16), wide(down.astype(BF16))])
        to_one = swap_pair(own, first, members)
        to_two = swap_pair(after(own, to_one), second, members)
        now = jnp.where(loses, jnp.where(is_one, to_one, to_two), own)
        return now[0], now[1]

    def halves(up, down):
        upper, lower = up.astype(BF16), wide(down.astype(BF16))

        to_one = swap_pair(upper, first, members)
        to_two = swap_pair(after(lower, to_one), second, members)
        mine = jnp.where(is_one, to_one, to_two)
        got = swap_pair(mine, third, members)
        return (
            jnp.where(loses, jnp.where(is_one, mine, got), upper),
            jnp.where(loses, jnp.where(is_one, got, mine), lower),
        )

    return lax.cond(shared, halves, whole, up, down)


def wide(value):
    half = value.shape[0] // 2
    return jnp.concatenate([value[:half], value[half:]], axis=1)


def take_through_all(value, source, members):
    flat = value.reshape(members, -1)
    parts = lax.all_to_all(flat, "member", split_axis=0, concat_axis=0, tiled=True)
    picked = jnp.take(parts, source, axis=0)
    return lax.all_to_all(picked, "member", split_axis=0, concat_axis=0, tiled=True).reshape(value.shape)


def swap_core(value):
    return lax.ppermute(value, "dp", [(0, 1), (1, 0), (2, 3), (3, 2)])


def swap_chip(value):
    return lax.ppermute(value, "dp", [(0, 2), (2, 0), (1, 3), (3, 1)])


TILE = 768
ROWS = 16


def gradient_kernel(
    images,
    patches,
    batch_total,
    place_ref,
    label_ref,
    tokens_hbm,
    classifier_hbm,
    up_own,
    up_near,
    up_far,
    up_diagonal,
    down_own,
    down_near,
    down_far,
    down_diagonal,
    own_out,
    near_out,
    far_out,
    diagonal_out,
    tokens_ref,
    classifier_ref,
    up_ref,
    down_ref,
    classes_ref,
    normed_ref,
    turned_ref,
    active_ref,
    slope_ref,
    residual_ref,
    inverse_ref,
    delta_ref,
    up_grad_ref,
    down_grad_ref,
    arrived,
    left,
):
    rows, features = residual_ref.shape
    hidden = up_ref.shape[1]
    share = up_own.shape[0]
    place = place_ref[0]
    up_scale = features ** (-0.5)
    down_scale = hidden ** (-0.5)

    tokens_copy = pltpu.make_async_copy(tokens_hbm, tokens_ref, arrived.at[12])
    classifier_copy = pltpu.make_async_copy(classifier_hbm, classifier_ref, arrived.at[13])
    tokens_copy.start()
    residual_ref[pl.ds(images * patches, rows - images * patches), :] = jnp.zeros(
        (rows - images * patches, features), F32
    )
    up_copies, down_copies = [], []
    for step, block in enumerate((up_own, up_near, up_far, up_diagonal)):
        at = pl.multiple_of((place ^ step) * share, share)
        up_copies.append(pltpu.make_async_copy(block, up_ref.at[pl.ds(at, share), :], arrived.at[step]))
    for step, block in enumerate((down_own, down_near, down_far, down_diagonal)):
        for half in range(2):
            at = pl.multiple_of((place ^ step) * (2 * share) + half * share, share)
            down_copies.append(
                pltpu.make_async_copy(
                    block.at[:, pl.ds(half * features, features)],
                    down_ref.at[pl.ds(at, share), :],
                    arrived.at[4 + 2 * step + half],
                )
            )
    for copy in up_copies + down_copies + [classifier_copy]:
        copy.start()

    tokens_copy.wait()
    for step in range(patches):
        residual_ref[pl.ds(step * images, images), :] = tokens_ref[step].astype(F32)

    def norm_rows(step, carry):
        here = pl.ds(pl.multiple_of(step * ROWS, ROWS), ROWS)
        value = residual_ref[here, :]
        center = value - jnp.mean(value, axis=1, keepdims=True)
        spread = jnp.mean(center * center, axis=1, keepdims=True)
        normed_ref[here, :] = (center * lax.rsqrt(spread + 1e-06)).astype(BF16)
        return carry

    lax.fori_loop(0, rows // ROWS, norm_rows, 0, unroll=True)
    turned_ref[...] = normed_ref[...].T
    for copy in up_copies:
        copy.wait()

    def up_tile(step, carry):
        here = pl.ds(pl.multiple_of(step * TILE, TILE), TILE)
        preact = jnp.dot(normed_ref[...], up_ref[:, here], preferred_element_type=F32) * up_scale
        half = 0.5 * (1.0 + lax.erf(preact * 0.7071067811865476))
        active_ref[:, here] = (preact * half).astype(BF16)
        slope_ref[:, here] = half + preact * jnp.exp(-0.5 * preact * preact) * 0.3989422804014327
        return carry

    lax.fori_loop(0, hidden // TILE, up_tile, 0, unroll=2)
    for copy in down_copies:
        copy.wait()

    product = jnp.dot(active_ref[...], down_ref[...], preferred_element_type=F32)
    residual_ref[...] += product * down_scale

    def norm_out(step, total):
        here = pl.ds(pl.multiple_of(step * ROWS, ROWS), ROWS)
        value = residual_ref[here, :]
        center = value - jnp.mean(value, axis=1, keepdims=True)
        spread = jnp.mean(center * center, axis=1, keepdims=True)
        inverse = lax.rsqrt(spread + 1e-06)
        out = center * inverse
        residual_ref[here, :] = out
        inverse_ref[here, :] = jnp.broadcast_to(inverse, (ROWS, inverse_ref.shape[1]))
        return total + out[:8] + out[8:]

    total = lax.fori_loop(0, rows // ROWS, norm_out, jnp.zeros((8, features), F32), unroll=True)
    fold = images
    while fold < 8:
        total = total + jnp.concatenate([total[fold:], total[:fold]], axis=0)
        fold *= 2
    pooled = (total * (1.0 / patches)).astype(BF16)
    classifier_copy.wait()
    classes = classifier_ref.shape[0]
    classes_ref[...] = jnp.zeros_like(classes_ref)
    classes_ref[:classes, :] = classifier_ref[...].astype(F32)
    heads = classes_ref[...].astype(BF16)
    logits = lax.dot_general(pooled, heads, (((1,), (1,)), ((), ())), preferred_element_type=F32)
    kind = lax.broadcasted_iota(jnp.int32, logits.shape, 1)
    image_row = lax.broadcasted_iota(jnp.int32, logits.shape, 0)
    powered = jnp.where(kind < classes, jnp.exp(logits), 0.0)
    softmax_out = powered / jnp.sum(powered, axis=1, keepdims=True)
    label = jnp.full(logits.shape, -1, jnp.int32)
    for image in range(images):
        label = jnp.where(image_row % images == image, label_ref[image], label)
    onehot = jnp.where(kind == label, 1.0, 0.0)
    logit_delta = ((softmax_out - onehot) * (1.0 / batch_total)).astype(BF16)
    pool_delta = jnp.dot(logit_delta, heads, preferred_element_type=F32) * (1.0 / patches)
    pool_center = pool_delta - jnp.mean(pool_delta, axis=1, keepdims=True)

    token_delta = jnp.concatenate([pool_delta, pool_delta], axis=0)
    token_center = jnp.concatenate([pool_center, pool_center], axis=0)

    def delta_rows(step, carry):
        here = pl.ds(pl.multiple_of(step * ROWS, ROWS), ROWS)
        out = residual_ref[here, :]
        along = jnp.mean(token_delta * out, axis=1, keepdims=True)
        inverse = inverse_ref[here, :][:, :1]
        delta_ref[here, :] = (inverse * (token_center - out * along)).astype(BF16)
        return carry

    lax.fori_loop(0, rows // ROWS, delta_rows, 0, unroll=True)

    def back_tile(step, carry):
        here = pl.ds(pl.multiple_of(step * TILE, TILE), TILE)
        down_grad_ref[here, :] = (
            lax.dot_general(
                active_ref[:, here], delta_ref[...], (((0,), (0,)), ((), ())), preferred_element_type=F32
            )
            * down_scale
        ).astype(BF16)
        hidden_delta = lax.dot_general(
            delta_ref[...], down_ref[here, :], (((1,), (1,)), ((), ())), preferred_element_type=F32
        )
        preact_delta = (hidden_delta * down_scale * slope_ref[:, here]).astype(BF16)
        active_ref[:, here] = preact_delta
        return carry

    lax.fori_loop(0, hidden // TILE, back_tile, 0, unroll=2)

    outputs = (own_out, near_out, far_out, diagonal_out)
    leaving = []
    for step, block in enumerate(outputs):
        for half in range(2):
            at = pl.multiple_of((place ^ step) * (2 * share) + half * share, share)
            leaving.append(
                pltpu.make_async_copy(
                    down_grad_ref.at[pl.ds(at, share), :],
                    block.at[1, :, pl.ds(half * features, features)],
                    left.at[len(leaving)],
                )
            )
            leaving[-1].start()
    for tile in range(hidden // TILE):
        here = pl.ds(tile * TILE, TILE)
        up_grad_ref[:, here] = (
            jnp.dot(turned_ref[...], active_ref[:, here], preferred_element_type=F32) * up_scale
        ).astype(BF16)
        for step, block in enumerate(outputs):
            at = pl.multiple_of((place ^ step) * share, share)
            leaving.append(
                pltpu.make_async_copy(
                    up_grad_ref.at[pl.ds(at, share), here], block.at[0, :, here], left.at[len(leaving)]
                )
            )
            leaving[-1].start()
    for copy in leaving:
        copy.wait()


def gradients(tokens, labels, place, shards, classifier, up_blocks, down_blocks):
    images, patches, features = tokens.shape
    share, hidden = up_blocks[0].shape
    rows = -(-images * patches // 64) * 64
    tokens = tokens.transpose(1, 0, 2)
    classifier = classifier.T
    in_smem = pl.BlockSpec(memory_space=pltpu.SMEM)
    anywhere = pl.BlockSpec(memory_space=pltpu.HBM)
    width = -(-classifier.shape[0] // 128) * 128
    return pl.pallas_call(
        lambda *refs: gradient_kernel(images, patches, images * shards, *refs),
        out_shape=[jax.ShapeDtypeStruct((2, share, hidden), BF16)] * 4,
        in_specs=[in_smem] * 2 + [anywhere] * 10,
        out_specs=[anywhere] * 4,
        scratch_shapes=[
            pltpu.VMEM(tokens.shape, BF16),
            pltpu.VMEM(classifier.shape, BF16),
            pltpu.VMEM((features, hidden), BF16),
            pltpu.VMEM((hidden, features), BF16),
            pltpu.VMEM((width, features), F32),
            pltpu.VMEM((rows, features), BF16),
            pltpu.VMEM((features, rows), BF16),
            pltpu.VMEM((rows, hidden), BF16),
            pltpu.VMEM((rows, hidden), F32),
            pltpu.VMEM((rows, features), F32),
            pltpu.VMEM((rows, 128), F32),
            pltpu.VMEM((rows, features), BF16),
            pltpu.VMEM((features, hidden), BF16),
            pltpu.VMEM((hidden, features), BF16),
            pltpu.SemaphoreType.DMA((14,)),
            pltpu.SemaphoreType.DMA((8 + 4 * (hidden // TILE),)),
        ],
        compiler_params=pltpu.CompilerParams(vmem_limit_bytes=56 * 1024 * 1024),
        cost_estimate=pl.CostEstimate(
            flops=10 * rows * features * hidden, bytes_accessed=12 * 1024 * 1024, transcendentals=0
        ),
    )(place.reshape(1), labels, tokens, classifier, *up_blocks, *down_blocks)


CHUNKS = 4


def adamw_kernel(candidates, choice_ref, rate_ref, decay_ref, *refs):
    near, away, own = refs[:3]
    sides = []
    at = 3
    for _ in range(2):
        sides.append(refs[at : at + 4 + candidates])
        at += 4 + candidates
    outputs = refs[at : at + 6]
    buffers = refs[at + 6 : -2]
    arrived, left = refs[-2:]

    def spots(kind, chunk):
        rows, columns = sides[kind][0].shape
        step = rows // CHUNKS
        here = (pl.ds(chunk * step, step), slice(None))
        if not kind:
            return here, here
        half, part = divmod(chunk, CHUNKS // 2)
        return here, (pl.ds(part * step, step), pl.ds(half * columns, columns))

    def copies(kind, chunk):
        param, first, second, short = sides[kind][:4]
        taken = sides[kind][4:]
        here, there = spots(kind, chunk)
        held = buffers[9 * kind : 9 * kind + 9]
        old, old_short, moment, variance, variance_short, terms_own, terms_near, terms_away = (
            buffer.at[here] for buffer in held[:8]
        )
        base = (kind * CHUNKS + chunk) * 6

        def copy(source, target, index):
            return pltpu.make_async_copy(source, target, arrived.at[base + index])

        fixed = [
            copy(own.at[(kind,) + there], terms_own, 3),
            copy(near.at[(kind,) + there], terms_near, 4),
            copy(away.at[(kind,) + there], terms_away, 5),
        ]
        kept = [copy(param.at[here], old, 0), copy(first.at[here], moment, 1), copy(second.at[here], variance, 2)]

        def moved(index):
            return [
                copy(short.at[there], old_short, 0),
                copy(taken[index].at[(0,) + there], moment, 1),
                copy(taken[index].at[(1,) + there], variance_short, 2),
            ]

        return fixed, kept, moved

    choices = [choice_ref[0], choice_ref[1]]
    work = [(kind, chunk) for kind in range(2) for chunk in range(CHUNKS)]
    for kind, chunk in work:
        fixed, kept, moved = copies(kind, chunk)

        @pl.when(choices[kind] == 0)
        def _():
            for copy in kept:
                copy.start()

        for index in range(candidates):

            @pl.when(choices[kind] == index + 1)
            def _():
                for copy in moved(index):
                    copy.start()

        for copy in fixed:
            copy.start()

    rate, decay = rate_ref[0], decay_ref[0]
    leaving = []
    for kind, chunk in work:
        fixed, kept, moved = copies(kind, chunk)

        @pl.when(choices[kind] == 0)
        def _():
            for copy in kept:
                copy.wait()

        @pl.when(choices[kind] != 0)
        def _():
            for copy in moved(0):
                copy.wait()

        for copy in fixed:
            copy.wait()
        here, _ = spots(kind, chunk)
        held = buffers[9 * kind : 9 * kind + 9]
        old, old_short, moment_in, variance_in, variance_short, terms_own, terms_near, terms_away, moment_out = held
        own_state = choices[kind] == 0
        before = jnp.where(own_state, old[here], old_short[here].astype(F32))
        variance = jnp.where(own_state, variance_in[here], variance_short[here].astype(F32))
        gradient = terms_own[here].astype(F32) + terms_near[here].astype(F32) + terms_away[here].astype(F32)
        moment = 0.9 * moment_in[here].astype(F32) + 0.1 * gradient
        variance = 0.999 * variance + 0.001 * gradient * gradient
        root = jnp.sqrt(variance * (1.0 / (1.0 - 0.999**STEP))) + 1e-08
        update = moment * (1.0 / (1.0 - 0.9**STEP)) / root + decay * before
        old[here] = before - rate * update
        moment_out[here] = moment.astype(BF16)
        variance_in[here] = variance
        for source, target in zip((old, moment_out, variance_in), outputs[3 * kind : 3 * kind + 3]):
            leaving.append(pltpu.make_async_copy(source.at[here], target.at[here], left.at[len(leaving)]))
            leaving[-1].start()
    for copy in leaving:
        copy.wait()


def adamw(choices, rate, decay, shares, sides):
    candidates = len(sides[0]) - 4
    in_smem = pl.BlockSpec(memory_space=pltpu.SMEM)
    anywhere = pl.BlockSpec(memory_space=pltpu.HBM)
    outputs, buffers = [], []
    for side in sides:
        shape = side[0].shape
        outputs += [jax.ShapeDtypeStruct(shape, kind) for kind in (F32, BF16, F32)]
        buffers += [pltpu.VMEM(shape, kind) for kind in (F32, BF16, BF16, F32) + (BF16,) * 5]
    count = 2 * CHUNKS
    return pl.pallas_call(
        lambda *refs: adamw_kernel(candidates, *refs),
        out_shape=outputs,
        in_specs=[in_smem] * 3 + [anywhere] * (3 + 2 * (4 + candidates)),
        out_specs=[anywhere] * 6,
        scratch_shapes=buffers + [pltpu.SemaphoreType.DMA((6 * count,)), pltpu.SemaphoreType.DMA((3 * count,))],
        compiler_params=pltpu.CompilerParams(vmem_limit_bytes=56 * 1024 * 1024),
        cost_estimate=pl.CostEstimate(
            flops=40 * sides[0][0].size, bytes_accessed=16 * 1024 * 1024, transcendentals=0
        ),
    )(choices, rate, decay, *shares, *sides[0], *sides[1])


def per_device(
    tokens,
    labels,
    source,
    learn_rate,
    weight_decay,
    classifier,
    up_param,
    up_first,
    up_second,
    down_param,
    down_first,
    down_second,
):
    members = lax.axis_size("member")
    me = lax.axis_index("member")
    place = lax.axis_index("dp")
    tokens, labels = tokens[0], labels[0]
    up_param, up_first, up_second = up_param[0], up_first[0], up_second[0]
    down_param, down_first, down_second = down_param[0], down_first[0], down_second[0]
    up_state = jnp.stack([up_first, up_second.astype(BF16)])
    down_state = jnp.stack([wide(down_first), wide(down_second.astype(BF16))])
    if members == DIRECT_MEMBERS:
        plan = find_plan(source, me)
        choices = plan[7]
        up_short, down_short = exchange_weights(up_param, down_param, plan, members)
    else:
        up_short = take_through_all(up_param.astype(BF16), source, members)
        down_short = take_through_all(wide(down_param.astype(BF16)), source, members)
        choices = jnp.where(source[me] != me, jnp.ones((2,), jnp.int32), 0)

    up_far, down_far = swap_chip(up_short), swap_chip(down_short)
    up_near, down_near = swap_core(up_short), swap_core(down_short)
    up_state, down_state = after((up_state, down_state), (up_short, down_short))
    if members == DIRECT_MEMBERS:
        halves = exchange_start(up_state, down_state, plan, members)
        up_far, down_far = after((up_far, down_far), halves)
    up_diagonal, down_diagonal = swap_core(up_far), swap_core(down_far)
    own_terms, near_terms, far_terms, diagonal_terms = gradients(
        tokens,
        labels,
        place,
        lax.axis_size("dp"),
        classifier,
        (up_short, up_near, up_far, up_diagonal),
        (down_short, down_near, down_far, down_diagonal),
    )
    from_diagonal = swap_core(diagonal_terms)
    from_near = swap_core(near_terms)
    away = (far_terms.astype(F32) + from_diagonal.astype(F32)).astype(BF16)
    shares = (from_near, swap_chip(away), own_terms)
    up_state, down_state = after((up_state, down_state), away)
    if members == DIRECT_MEMBERS:
        to_one, to_two = halves
        to_third, to_fourth = exchange_finish(up_state, down_state, halves, plan, members)
        up_candidates, down_candidates = (to_one, to_two, to_third), (to_third, to_two, to_fourth)
    else:
        up_candidates = (take_through_all(up_state, source, members),)
        down_candidates = (take_through_all(down_state, source, members),)

    new_state = adamw(
        choices,
        learn_rate,
        weight_decay,
        shares,
        (
            (up_param, up_first, up_second, up_short, *up_candidates),
            (down_param, down_first, down_second, down_short, *down_candidates),
        ),
    )
    return tuple(part[None] for part in new_state)


def solution(mesh):
    rows = P("member", "dp", None)
    placed = (
        P("member", "dp", None, None),
        P("member", "dp"),
        P(),
        P("member"),
        P("member"),
        P(),
        rows,
        rows,
        rows,
        rows,
        rows,
        rows,
    )
    return jax.shard_map(per_device, mesh=mesh, in_specs=placed, out_specs=(rows,) * 6, check_vma=False)
```
